32 devices in a mesh: grp: 2 (over x), tile: 16 (over z, y, core).
Axes of the slice: x: 2, y: 2, z: 4, core: 2. Of those that a mesh axis runs over, the one named last changes fastest.
Arguments:
- full_resolution_frames: bfloat16 [32, 2, 512, 512], P(('grp', 'tile')), parts along dimension 0, may hold values from -24 to 24
- height_angle_factor: float32 [1024, 512], P('grp'), parts along dimension 0, may hold values from -4 to 4
- normal_spacings: float32 [32], P('grp'), parts along dimension 0, may hold values from -2 to 2
- couple_entry_flags: int32 [16, 3], replicated, may hold values from 0 to 1, as said below
- block_target_indices: int32 [32, 64], P('grp'), parts along dimension 0, may hold values from 0 to 255, as said below
- block_target_totals: int32 [32], P('grp'), parts along dimension 0, may hold values from 1 to 64, as said below
Outputs:
- coherence: float32 [32, 3, 128, 32], P(('grp', 'tile')), parts along dimension 0
- velocities: float32 [2048, 15], P(('grp', 'tile')), parts along dimension 0
The draws below stay inside these ranges and needn't reach their ends.
There are 2 independent parts, one for each index of `grp`. The reference program is written for one: setup_inputs(seed, part) draws one part's arguments, and reference() takes and returns one part's arrays. A program takes and returns all parts, laid end to end along the dimension named above; an argument that names none is the same for every part. Nothing has to cross between parts.
Inputs may be any that keep to these rules, and one draw needn't show every extreme that they name: `couple_entry_flags`: slot k-1 of date d stands for the pair of d and d + k; slot 0 is 1 wherever d + 1 < 16; slots with d + k >= 16 are 0. `block_target_indices`: row t lists distinct looked pixels of tile t; entries at or past the tile's count are 0. `block_target_totals`: some tile has exactly 64.
All inputs are finite; a program needn't handle non-finite values.
Results may differ from the reference program's by a relative error of at most 0.0003.
Values may be sent and summed in bfloat16 or wider, within the bound.
A program may use at most 192 MiB of HBM per device.

```python
import jax
import jax.numpy as jnp
from jax import lax

COLS = 512
SCAT_CAP = 64
LOOK_ROWS = 4
LOOK_COLS = 16
LATER_MATES = 3
DATES = 16
INTERVALS = 15
PAIRS = 48
ROWS = 512
TILE_PIX = 256
N_TILE = 16


def frame_fields(key):
    keys = jax.random.split(jax.random.fold_in(key, 11), 8)
    topo = jax.random.truncated_normal(keys[0], -4.0, 4.0, (ROWS, COLS), jnp.float32)
    baseline = jax.random.uniform(keys[1], (DATES,), jnp.float32, -2.0, 2.0)
    return (topo, baseline, keys)


def draw_height_angle_factor(key, part):
    topo, baseline, keys = frame_fields(key)
    return topo


def draw_normal_spacings(key, part):
    topo, baseline, keys = frame_fields(key)
    return baseline


def draw_full_resolution_frames(key, part):
    topo, baseline, keys = frame_fields(key)
    rate = jax.random.uniform(keys[2], (ROWS, COLS), jnp.float32, -3.0, 3.0)
    common_real = jax.random.truncated_normal(keys[3], -4.0, 4.0, (ROWS, COLS), jnp.float32)
    common_imag = jax.random.truncated_normal(keys[4], -4.0, 4.0, (ROWS, COLS), jnp.float32)
    sigma = jnp.exp(jax.random.uniform(keys[5], (DATES,), jnp.float32, jnp.log(0.3), jnp.log(3.0)))
    noise_real = jax.random.truncated_normal(keys[6], -4.0, 4.0, (DATES, ROWS, COLS), jnp.float32)
    noise_imag = jax.random.truncated_normal(keys[7], -4.0, 4.0, (DATES, ROWS, COLS), jnp.float32)
    times = jnp.arange(DATES, dtype=jnp.float32) / DATES
    angle = baseline[:, None, None] * topo[None] + times[:, None, None] * rate[None]
    cosine = jnp.cos(angle)
    sine = jnp.sin(angle)
    real_part = common_real[None] * cosine - common_imag[None] * sine + sigma[:, None, None] * noise_real
    imag_part = common_real[None] * sine + common_imag[None] * cosine + sigma[:, None, None] * noise_imag
    stacked = jnp.stack([real_part, imag_part], axis=1)
    stacked = jnp.clip(stacked, -24.0, 24.0)
    return stacked.astype(jnp.bfloat16)


def draw_couple_entry_flags(key, part):
    bits = jax.random.randint(key, (DATES, LATER_MATES), 0, 2, jnp.int32)
    slot = jnp.arange(LATER_MATES, dtype=jnp.int32)[None, :]
    dated = jnp.arange(DATES, dtype=jnp.int32)[:, None]
    chosen = jnp.where(slot == 0, 1, bits)
    return jnp.where(dated + slot + 1 < DATES, chosen, 0).astype(jnp.int32)


def scatter_lists(key):
    keys = jax.random.split(jax.random.fold_in(key, 23), 3)
    orders = jax.vmap(lambda single: jax.random.permutation(single, TILE_PIX))(jax.random.split(keys[0], N_TILE))
    orders = orders[:, :SCAT_CAP].astype(jnp.int32)
    counts = jax.random.randint(keys[1], (N_TILE,), 1, SCAT_CAP + 1, jnp.int32)
    fullest = jax.random.randint(keys[2], (), 0, N_TILE, jnp.int32)
    counts = jnp.where(jnp.arange(N_TILE, dtype=jnp.int32) == fullest, SCAT_CAP, counts)
    listed = jnp.where(jnp.arange(SCAT_CAP, dtype=jnp.int32)[None, :] < counts[:, None], orders, 0)
    return (listed.astype(jnp.int32), counts.astype(jnp.int32))


def draw_block_target_indices(key, part):
    listed, counts = scatter_lists(key)
    return listed


def draw_block_target_totals(key, part):
    listed, counts = scatter_lists(key)
    return counts


def setup_inputs(seed: int = 0, part: int = 0) -> dict:
    key_of = jax.random.split(jax.random.key(seed), 7)
    part_splits = jax.random.split(jax.random.fold_in(key_of[6], part), 7)
    full_resolution_frames = draw_full_resolution_frames(jax.random.fold_in(jax.random.fold_in(key_of[6], part), 71), part)
    height_angle_factor = draw_height_angle_factor(jax.random.fold_in(jax.random.fold_in(key_of[6], part), 71), part)
    normal_spacings = draw_normal_spacings(jax.random.fold_in(jax.random.fold_in(key_of[6], part), 71), part)
    couple_entry_flags = draw_couple_entry_flags(jax.random.fold_in(key_of[6], 71), part)
    block_target_indices = draw_block_target_indices(jax.random.fold_in(jax.random.fold_in(key_of[6], part), 71), part)
    block_target_totals = draw_block_target_totals(jax.random.fold_in(jax.random.fold_in(key_of[6], part), 71), part)
    return {"full_resolution_frames": full_resolution_frames, "height_angle_factor": height_angle_factor, "normal_spacings": normal_spacings, "couple_entry_flags": couple_entry_flags, "block_target_indices": block_target_indices, "block_target_totals": block_target_totals}


EPSILON = 1e-06

def looked(field):
    rows = field.shape[-2]
    cols = field.shape[-1]
    grid = field.reshape(field.shape[:-2] + (rows // LOOK_ROWS, LOOK_ROWS, cols // LOOK_COLS, LOOK_COLS))
    return lax.optimization_barrier(jnp.mean(grid, axis=(-3, -1)))

def pair_stats(own_real, own_imag, other_real, other_imag, theta):
    cross_real = own_real * other_real + own_imag * other_imag
    cross_imag = own_imag * other_real - own_real * other_imag
    cosine = jnp.cos(theta)
    sine = jnp.sin(theta)
    flat_real = cross_real * cosine + cross_imag * sine
    flat_imag = cross_imag * cosine - cross_real * sine
    mean_real = looked(flat_real)
    mean_imag = looked(flat_imag)
    power_own = looked(own_real * own_real + own_imag * own_imag)
    power_other = looked(other_real * other_real + other_imag * other_imag)
    scale = 1.0 / jnp.sqrt(power_own * power_other + EPSILON)
    return (jnp.sqrt(mean_real * mean_real + mean_imag * mean_imag) * scale, mean_imag * scale)

def inverse_map(couple_entry_flags):
    dates = couple_entry_flags.shape[0]
    later_mates = couple_entry_flags.shape[1]
    count = dates * later_mates
    pair_index = jnp.arange(count, dtype=jnp.int32)
    first_date = pair_index // later_mates
    pair_span = pair_index % later_mates + 1
    interval_index = jnp.arange(dates - 1, dtype=jnp.int32)
    covered = (interval_index[None, :] >= first_date[:, None]) & (interval_index[None, :] < (first_date + pair_span)[:, None])
    design = couple_entry_flags.reshape(count).astype(jnp.float32)[:, None] * covered.astype(jnp.float32)
    normal = jnp.dot(design.T, design, precision=lax.Precision.HIGHEST)
    return jnp.linalg.solve(normal, design.T)

def reference(full_resolution_frames, height_angle_factor, normal_spacings, couple_entry_flags, block_target_indices, block_target_totals):
    padded = jnp.concatenate([full_resolution_frames, jnp.zeros((LATER_MATES, 2, ROWS, COLS), full_resolution_frames.dtype)], axis=0)
    spacing_extended = jnp.concatenate([normal_spacings, jnp.zeros((LATER_MATES,), normal_spacings.dtype)], axis=0)

    def one_date(date):
        own = lax.dynamic_index_in_dim(padded, date, 0, keepdims=False).astype(jnp.float32)
        reference_spacing = lax.dynamic_index_in_dim(spacing_extended, date, 0, keepdims=False)
        cohs = []
        phases = []
        for offset in range(1, LATER_MATES + 1):
            other = lax.dynamic_index_in_dim(padded, date + offset, 0, keepdims=False).astype(jnp.float32)
            other_base = lax.dynamic_index_in_dim(spacing_extended, date + offset, 0, keepdims=False)
            theta = (reference_spacing - other_base) * height_angle_factor
            coh, phase = pair_stats(own[0], own[1], other[0], other[1], theta)
            cohs.append(coh)
            phases.append(phase)
        return (jnp.stack(cohs, axis=0), jnp.stack(phases, axis=0))
    cohs, phases = lax.map(one_date, jnp.arange(DATES, dtype=jnp.int32))
    coherence = cohs * couple_entry_flags.astype(jnp.float32)[:, :, None, None]
    phase_tiles = phases.reshape(PAIRS, N_TILE, TILE_PIX)
    picked = jnp.take_along_axis(phase_tiles, block_target_indices[None, :, :], axis=2)
    mapping = inverse_map(couple_entry_flags)
    velocities = jnp.einsum('ip,ptj->tji', mapping, picked, precision=lax.Precision.HIGHEST)
    valid = (jnp.arange(SCAT_CAP, dtype=jnp.int32)[None, :] < block_target_totals[:, None]).astype(jnp.float32)
    velocities = velocities * valid[:, :, None]
    return (coherence, velocities.reshape(N_TILE * SCAT_CAP, INTERVALS))
```

```python
import functools

import jax
import jax.numpy as jnp
from jax import lax
from jax.experimental import pallas as pl
from jax.experimental.pallas import tpu as pltpu
from jax.sharding import PartitionSpec as P

LOOK_ROWS = 4
LOOK_COLS = 16
LANES = 128
EPSILON = 1e-06
HIGHEST = lax.Precision.HIGHEST


def iota(shape, axis):
    return lax.broadcasted_iota(jnp.int32, shape, axis)


def sine_cosine(x):
    turns = jnp.round(x * 0.6366197723675814)
    r = (x - turns * 1.5703125) - turns * 4.838267948966e-4
    z = r * r
    s = r + r * z * (-1.6666654611e-1 + z * (8.3321608736e-3 + z * -1.9515295891e-4))
    c = 1.0 - 0.5 * z + z * z * (
        4.166664568298827e-2 + z * (-1.388731625493765e-3 + z * 2.443315711809948e-5)
    )
    quarter = turns.astype(jnp.int32)
    odd = (quarter & 1) == 1
    sine = jnp.where(odd, c, s) * (1 - (quarter & 2)).astype(jnp.float32)
    cosine = jnp.where(odd, s, c) * (1 - ((quarter + 1) & 2)).astype(jnp.float32)
    return sine, cosine


def inverse_map(flags, dates, mates):
    intervals = dates - 1
    rows = -(-intervals // 8) * 8
    pairs = -(-dates * mates // LANES) * LANES
    slot = iota((dates, pairs), 1)
    spread = jnp.zeros((dates, pairs), jnp.float32)
    for k in range(mates):
        spread = spread + jnp.where(slot % mates == k, flags[:, k : k + 1].astype(jnp.float32), 0.0)
    used = jnp.sum(
        jnp.where(slot // mates == iota((dates, pairs), 0), spread, 0.0), axis=0, keepdims=True
    )
    interval = iota((rows, pairs), 0)
    pair = iota((rows, pairs), 1)
    first = pair // mates
    covered = (interval >= first) & (interval < first + pair % mates + 1) & (interval < intervals)
    right = jnp.where(covered, used, 0.0)
    normal = lax.dot_general(
        right.astype(jnp.bfloat16),
        right.astype(jnp.bfloat16),
        (((1,), (1,)), ((), ())),
        preferred_element_type=jnp.float32,
    )
    down = iota((rows, rows), 0)
    across = iota((rows, rows), 1)
    down_right = iota((rows, pairs), 0)

    def eliminate(t, carry):
        a, b = carry
        row_a = jnp.sum(jnp.where(down == t, a, 0.0), axis=0, keepdims=True)
        row_b = jnp.sum(jnp.where(down_right == t, b, 0.0), axis=0, keepdims=True)
        column = jnp.sum(jnp.where(across == t, a, 0.0), axis=1, keepdims=True)
        pivot = jnp.sum(jnp.where(across[:1] == t, row_a, 0.0), axis=1, keepdims=True)
        row_a = row_a / pivot
        row_b = row_b / pivot
        return (
            jnp.where(down == t, row_a, a - column * row_a),
            jnp.where(down_right == t, row_b, b - column * row_b),
        )

    return lax.fori_loop(0, intervals, eliminate, (normal, right))[1]


def kernel(
    dates,
    mates,
    frames,
    heights,
    spacings,
    flags_scalar,
    flags_vector,
    targets,
    totals,
    coherence,
    velocities,
    held,
    height_rows,
    natural,
    height_looks,
    rotated,
    powers,
    phases,
    coh,
    send_sem,
    recv_sem,
    coh_send_sem,
    coh_recv_sem,
    local_sem,
):
    me = lax.axis_index("tile")
    rows = held.shape[2]
    cols = held.shape[3]
    tiles = cols // LANES
    looks = rows // LOOK_ROWS
    looked_cols = cols // LOOK_COLS
    pairs = dates * mates
    slots = targets.shape[1]
    window = rotated.shape[0]

    own_rows = pl.ds(pl.multiple_of(me * rows, rows), rows)
    own_block = pltpu.make_async_copy(frames.at[0, :, own_rows, :], held.at[me], local_sem.at[0])
    own_heights = pltpu.make_async_copy(heights.at[own_rows, :], height_rows, local_sem.at[1])
    own_block.start()
    own_heights.start()

    barrier = pltpu.get_barrier_semaphore()

    def greet(step, carry):
        pl.semaphore_signal(
            barrier,
            inc=1,
            device_id={"tile": (me + step) % dates},
            device_id_type=pl.DeviceIdType.MESH,
        )
        return carry

    lax.fori_loop(1, dates, greet, 0)
    pl.semaphore_wait(barrier, dates - 1)

    def image_copy(to, date):
        return pltpu.make_async_remote_copy(
            src_ref=frames.at[0, :, pl.ds(pl.multiple_of(to * rows, rows), rows), :],
            dst_ref=held.at[date],
            send_sem=send_sem.at[to],
            recv_sem=recv_sem.at[date],
            device_id={"tile": to},
            device_id_type=pl.DeviceIdType.MESH,
        )

    def send_image(step, carry):
        image_copy((me + step) % dates, me).start()
        return carry

    lax.fori_loop(1, dates, send_image, 0)

    def coh_copy(to, tile):
        return pltpu.make_async_remote_copy(
            src_ref=coh.at[to],
            dst_ref=coherence.at[0, :, pl.ds(pl.multiple_of(tile * looks, looks), looks), :],
            send_sem=coh_send_sem.at[to],
            recv_sem=coh_recv_sem.at[tile],
            device_id={"tile": to},
            device_id_type=pl.DeviceIdType.MESH,
        )

    own_coh = pltpu.make_async_copy(
        coh.at[me],
        coherence.at[0, :, pl.ds(pl.multiple_of(me * looks, looks), looks), :],
        local_sem.at[2],
    )

    def hand_out(date):
        @pl.when(date == me)
        def _():
            own_coh.start()

        @pl.when(date != me)
        def _():
            coh_copy(date, me).start()

    rotated[...] = jnp.zeros_like(rotated)
    powers[...] = jnp.zeros_like(powers)
    phases[...] = jnp.zeros_like(phases)
    coh[...] = jnp.zeros_like(coh)

    mapping = inverse_map(flags_vector[...], dates, mates)

    look_lane = iota((cols, LANES), 1)
    pooling = jnp.where(
        iota((cols, LANES), 0) // LOOK_COLS == look_lane, 1.0 / (LOOK_ROWS * LOOK_COLS), 0.0
    ).astype(jnp.bfloat16)

    own_block.wait()
    own_heights.wait()
    for c in range(tiles):
        natural[0, c] = height_rows[:, c * LANES : (c + 1) * LANES]
    for j in range(LOOK_ROWS):
        height_looks[j] = natural[0, :, pl.ds(j, looks, stride=LOOK_ROWS), :]

    def one_date(date, carry):
        @pl.when(date != me)
        def _():
            image_copy(date, date).wait_recv()

        place = date % window
        for plane in range(2):
            for c in range(tiles):
                natural[plane, c] = held[date, plane, :, c * LANES : (c + 1) * LANES].astype(
                    jnp.float32
                )
        spacing = spacings[date]
        power = None
        for j in range(LOOK_ROWS):
            real = natural[0, :, pl.ds(j, looks, stride=LOOK_ROWS), :]
            imag = natural[1, :, pl.ds(j, looks, stride=LOOK_ROWS), :]
            sine, cosine = sine_cosine(spacing * height_looks[j])
            rotated[place, 0, j] = real * cosine + imag * sine
            rotated[place, 1, j] = imag * cosine - real * sine
            energy = real * real + imag * imag
            power = energy if j == 0 else power + energy
        fields = [power]
        for k in range(1, mates + 1):
            other = (date + window - k) % window
            flat_real = 0.0
            flat_imag = 0.0
            for j in range(LOOK_ROWS):
                a_real = rotated[other, 0, j]
                a_imag = rotated[other, 1, j]
                c_real = rotated[place, 0, j]
                c_imag = rotated[place, 1, j]
                flat_real = flat_real + (a_real * c_real + a_imag * c_imag)
                flat_imag = flat_imag + (a_imag * c_real - a_real * c_imag)
            fields += [flat_real, flat_imag]
        sums = jnp.concatenate(
            [jnp.concatenate([field[c] for c in range(tiles)], axis=1) for field in fields], axis=0
        )
        high = sums.astype(jnp.bfloat16).astype(jnp.float32)
        split = jnp.concatenate([high, sums - high], axis=0).astype(jnp.bfloat16)
        pooled = jnp.dot(split, pooling, preferred_element_type=jnp.float32)
        means = pooled[: sums.shape[0]] + pooled[sums.shape[0] :]
        power_other = means[:looks]
        powers[place] = power_other
        for k in range(1, mates + 1):
            mean_real = means[(2 * k - 1) * looks : 2 * k * looks]
            mean_imag = means[2 * k * looks : (2 * k + 1) * looks]
            power_own = powers[(date + window - k) % window]
            scale = 1.0 / jnp.sqrt(power_own * power_other + EPSILON)
            amplitude = jnp.sqrt(mean_real * mean_real + mean_imag * mean_imag) * scale

            @pl.when(date >= k)
            def _():
                flag = flags_scalar[date - k, k - 1].astype(jnp.float32)
                coh[date - k, k - 1] = (amplitude * flag)[:, :looked_cols]
                phases[(date - k) * mates + (k - 1)] = mean_imag * scale

        @pl.when(date >= mates)
        def _():
            hand_out(date - mates)

        return carry

    lax.fori_loop(0, dates, one_date, 0)
    lax.fori_loop(dates - mates, dates, lambda date, carry: (hand_out(date), carry)[1], 0)

    listed = targets[pl.ds(me, 1), :]
    diagonal = iota((slots, slots), 0) == iota((slots, slots), 1)
    row_of = (listed // looked_cols).astype(jnp.float32)
    column_of = (listed % looked_cols).astype(jnp.float32)
    row_down = jnp.sum(jnp.where(diagonal, row_of, 0.0), axis=1, keepdims=True)
    column_down = jnp.sum(jnp.where(diagonal, column_of, 0.0), axis=1, keepdims=True)
    by_column = jnp.where(
        iota((slots, LANES), 1).astype(jnp.float32) == column_down, 1.0, 0.0
    )
    flat_phases = phases[...].reshape(pairs * looks, LANES)
    rows_picked = lax.dot_general(
        by_column,
        flat_phases,
        (((1,), (1,)), ((), ())),
        precision=HIGHEST,
        preferred_element_type=jnp.float32,
    )
    lane = iota((slots, pairs * looks), 1)
    picked = jnp.where((lane % looks).astype(jnp.float32) == row_down, rows_picked, 0.0)
    expand = jnp.where(
        iota((mapping.shape[1], pairs * looks), 1) // looks
        == iota((mapping.shape[1], pairs * looks), 0),
        1.0,
        0.0,
    )
    wide = jnp.dot(mapping, expand, precision=HIGHEST, preferred_element_type=jnp.float32)
    result = lax.dot_general(
        picked,
        wide,
        (((1,), (1,)), ((), ())),
        precision=HIGHEST,
        preferred_element_type=jnp.float32,
    )
    result = jnp.where(iota(result.shape, 0) < totals[me], result, 0.0)
    velocities[...] = result[:, : dates - 1]

    own_coh.wait()

    def finish(step, carry):
        other = (me + step) % dates
        image_copy(other, me).wait_send()
        coh_copy(other, me).wait_send()
        coh_copy(other, other).wait_recv()
        return carry

    lax.fori_loop(1, dates, finish, 0)


def local(
    full_resolution_frames,
    height_angle_factor,
    normal_spacings,
    couple_entry_flags,
    block_target_indices,
    block_target_totals,
):
    dates, mates = couple_entry_flags.shape
    image_rows, cols = height_angle_factor.shape
    rows = image_rows // dates
    tiles = cols // LANES
    looks = rows // LOOK_ROWS
    looked_cols = cols // LOOK_COLS
    slots = block_target_indices.shape[1]
    window = mates + 1
    f32 = jnp.float32
    vmem = pl.BlockSpec(memory_space=pltpu.VMEM)
    smem = pl.BlockSpec(memory_space=pltpu.SMEM)
    anywhere = pl.BlockSpec(memory_space=pl.ANY)
    return pl.pallas_call(
        functools.partial(kernel, dates, mates),
        out_shape=(
            jax.ShapeDtypeStruct((1, mates, image_rows // LOOK_ROWS, looked_cols), f32),
            jax.ShapeDtypeStruct((slots, dates - 1), f32),
        ),
        in_specs=[anywhere, anywhere, smem, smem, vmem, vmem, smem],
        out_specs=(vmem, vmem),
        scratch_shapes=[
            pltpu.VMEM((dates, 2, rows, cols), jnp.bfloat16),
            pltpu.VMEM((rows, cols), f32),
            pltpu.VMEM((2, tiles, rows, LANES), f32),
            pltpu.VMEM((LOOK_ROWS, tiles, looks, LANES), f32),
            pltpu.VMEM((window, 2, LOOK_ROWS, tiles, looks, LANES), f32),
            pltpu.VMEM((window, looks, LANES), f32),
            pltpu.VMEM((dates * mates, looks, LANES), f32),
            pltpu.VMEM((dates, mates, looks, looked_cols), f32),
            pltpu.SemaphoreType.DMA((dates,)),
            pltpu.SemaphoreType.DMA((dates,)),
            pltpu.SemaphoreType.DMA((dates,)),
            pltpu.SemaphoreType.DMA((dates,)),
            pltpu.SemaphoreType.DMA((3,)),
        ],
        compiler_params=pltpu.CompilerParams(
            collective_id=0, has_side_effects=True, vmem_limit_bytes=40 * 1024 * 1024
        ),
    )(
        full_resolution_frames,
        height_angle_factor,
        normal_spacings,
        couple_entry_flags,
        couple_entry_flags,
        block_target_indices,
        block_target_totals,
    )


def solution(mesh):
    in_specs = (
        P(("grp", "tile"), None, None, None),
        P("grp", None),
        P("grp"),
        P(),
        P("grp", None),
        P("grp"),
    )
    out_specs = (P(("grp", "tile"), None, None, None), P(("grp", "tile"), None))
    return jax.shard_map(local, mesh=mesh, in_specs=in_specs, out_specs=out_specs, check_vma=False)
```

```python
import functools

import jax
import jax.numpy as jnp
from jax import lax
from jax.experimental import pallas as pl
from jax.experimental.pallas import tpu as pltpu
from jax.sharding import PartitionSpec as P

LOOK_ROWS = 4
LOOK_COLS = 16
LANES = 128
EPSILON = 1e-06
HIGHEST = lax.Precision.HIGHEST


def iota(shape, axis):
    return lax.broadcasted_iota(jnp.int32, shape, axis)


def sine_cosine(x):
    turns = jnp.round(x * 0.6366197723675814)
    r = (x - turns * 1.5703125) - turns * 4.838267948966e-4
    z = r * r
    s = r + r * z * (-1.6666654611e-1 + z * (8.3321608736e-3 + z * -1.9515295891e-4))
    c = 1.0 - 0.5 * z + z * z * (
        4.166664568298827e-2 + z * (-1.388731625493765e-3 + z * 2.443315711809948e-5)
    )
    quarter = turns.astype(jnp.int32)
    odd = (quarter & 1) == 1
    sine = jnp.where(odd, c, s) * (1 - (quarter & 2)).astype(jnp.float32)
    cosine = jnp.where(odd, s, c) * (1 - ((quarter + 1) & 2)).astype(jnp.float32)
    return sine, cosine


def inverse_map(flags, dates, mates):
    intervals = dates - 1
    rows = -(-intervals // 8) * 8
    pairs = -(-dates * mates // LANES) * LANES
    own_slot = iota((dates, pairs), 1) // mates == iota((dates, pairs), 0)
    spread = jnp.dot(
        flags.astype(jnp.bfloat16),
        jnp.where(own_slot, 1.0, 0.0).astype(jnp.bfloat16),
        preferred_element_type=jnp.float32,
    )
    kind = iota((mates, pairs), 1) % mates == iota((mates, pairs), 0)
    used = jnp.sum(jnp.where(kind, spread, 0.0), axis=0, keepdims=True)
    interval = iota((rows, pairs), 0)
    pair = iota((rows, pairs), 1)
    first = pair // mates
    covered = (interval >= first) & (interval < first + pair % mates + 1) & (interval < intervals)
    right = jnp.where(covered, used, 0.0)
    normal = lax.dot_general(
        right.astype(jnp.bfloat16),
        right.astype(jnp.bfloat16),
        (((1,), (1,)), ((), ())),
        preferred_element_type=jnp.float32,
    )
    down = iota((rows, rows), 0)
    across = iota((rows, rows), 1)
    down_right = iota((rows, pairs), 0)

    def eliminate(t, carry):
        a, b = carry
        row_a = jnp.sum(jnp.where(down == t, a, 0.0), axis=0, keepdims=True)
        row_b = jnp.sum(jnp.where(down_right == t, b, 0.0), axis=0, keepdims=True)
        column = jnp.sum(jnp.where(across == t, a, 0.0), axis=1, keepdims=True)
        pivot = jnp.sum(jnp.where(across[:1] == t, row_a, 0.0), axis=1, keepdims=True)
        row_a = row_a / pivot
        row_b = row_b / pivot
        return (
            jnp.where(down == t, row_a, a - column * row_a),
            jnp.where(down_right == t, row_b, b - column * row_b),
        )

    return lax.fori_loop(0, intervals, eliminate, (normal, right))[1]


def kernel(
    dates,
    mates,
    frames,
    heights,
    spacings,
    flags_scalar,
    flags_vector,
    targets,
    totals,
    coherence,
    velocities,
    held,
    height_rows,
    natural,
    height_looks,
    rotated,
    powers,
    phases,
    coh,
    gathered,
    send_sem,
    recv_sem,
    coh_send_sem,
    coh_recv_sem,
    local_sem,
):
    me = lax.axis_index("tile")
    rows = held.shape[2]
    cols = held.shape[3]
    tiles = cols // LANES
    looks = rows // LOOK_ROWS
    looked_cols = cols // LOOK_COLS
    pairs = dates * mates
    slots = targets.shape[1]
    window = rotated.shape[0]

    own_rows = pl.ds(pl.multiple_of(me * rows, rows), rows)
    own_block = pltpu.make_async_copy(frames.at[0, :, own_rows, :], held.at[me], local_sem.at[0])
    own_heights = pltpu.make_async_copy(heights.at[own_rows, :], height_rows, local_sem.at[1])
    own_block.start()
    own_heights.start()

    barrier = pltpu.get_barrier_semaphore()

    def greet(step, carry):
        pl.semaphore_signal(
            barrier,
            inc=1,
            device_id={"tile": (me + step) % dates},
            device_id_type=pl.DeviceIdType.MESH,
        )
        return carry

    lax.fori_loop(1, dates, greet, 0)
    pl.semaphore_wait(barrier, dates - 1)

    def partner(step):
        return me ^ step if dates & (dates - 1) == 0 else (me + step) % dates

    def image_copy(to, date):
        return pltpu.make_async_remote_copy(
            src_ref=frames.at[0, :, pl.ds(pl.multiple_of(to * rows, rows), rows), :],
            dst_ref=held.at[date],
            send_sem=send_sem.at[to],
            recv_sem=recv_sem.at[date],
            device_id={"tile": to},
            device_id_type=pl.DeviceIdType.MESH,
        )

    def send_image(step, carry):
        image_copy(partner(dates - step), me).start()
        return carry

    lax.fori_loop(1, dates, send_image, 0)

    def coh_copy(to, tile):
        return pltpu.make_async_remote_copy(
            src_ref=coh.at[to],
            dst_ref=gathered.at[pl.ds(pl.multiple_of(tile * looks, looks), looks), :],
            send_sem=coh_send_sem.at[to],
            recv_sem=coh_recv_sem.at[tile],
            device_id={"tile": to},
            device_id_type=pl.DeviceIdType.MESH,
        )

    own_coh = pltpu.make_async_copy(
        coh.at[me],
        gathered.at[pl.ds(pl.multiple_of(me * looks, looks), looks), :],
        local_sem.at[2],
    )

    def hand_out(date):
        @pl.when(date == me)
        def _():
            own_coh.start()

        @pl.when(date != me)
        def _():
            coh_copy(date, me).start()

    rotated[...] = jnp.zeros_like(rotated)
    powers[...] = jnp.zeros_like(powers)
    phases[...] = jnp.zeros_like(phases)
    coh[...] = jnp.zeros_like(coh)
    assert mates * looked_cols <= LANES

    mapping = inverse_map(flags_vector[...], dates, mates)

    look_lane = iota((cols, LANES), 1)
    pooling = jnp.where(
        iota((cols, LANES), 0) // LOOK_COLS == look_lane, 1.0 / (LOOK_ROWS * LOOK_COLS), 0.0
    ).astype(jnp.bfloat16)

    own_block.wait()
    own_heights.wait()
    for c in range(tiles):
        natural[0, c] = height_rows[:, c * LANES : (c + 1) * LANES]
    for j in range(LOOK_ROWS):
        height_looks[j] = natural[0, :, pl.ds(j, looks, stride=LOOK_ROWS), :]

    def one_date(date, carry):
        @pl.when(date != me)
        def _():
            image_copy(date, date).wait_recv()

        place = date % window
        for plane in range(2):
            for c in range(tiles):
                natural[plane, c] = held[date, plane, :, c * LANES : (c + 1) * LANES].astype(
                    jnp.float32
                )
        spacing = spacings[date]
        power = None
        for j in range(LOOK_ROWS):
            real = natural[0, :, pl.ds(j, looks, stride=LOOK_ROWS), :]
            imag = natural[1, :, pl.ds(j, looks, stride=LOOK_ROWS), :]
            sine, cosine = sine_cosine(spacing * height_looks[j])
            rotated[place, 0, j] = real * cosine + imag * sine
            rotated[place, 1, j] = imag * cosine - real * sine
            energy = real * real + imag * imag
            power = energy if j == 0 else power + energy
        fields = [power]
        for k in range(1, mates + 1):
            other = (date + window - k) % window
            flat_real = 0.0
            flat_imag = 0.0
            for j in range(LOOK_ROWS):
                a_real = rotated[other, 0, j]
                a_imag = rotated[other, 1, j]
                c_real = rotated[place, 0, j]
                c_imag = rotated[place, 1, j]
                flat_real = flat_real + (a_real * c_real + a_imag * c_imag)
                flat_imag = flat_imag + (a_imag * c_real - a_real * c_imag)
            fields += [flat_real, flat_imag]
        sums = jnp.concatenate(
            [jnp.concatenate([field[c] for c in range(tiles)], axis=1) for field in fields], axis=0
        )
        high = sums.astype(jnp.bfloat16).astype(jnp.float32)
        split = jnp.concatenate([high, sums - high], axis=0).astype(jnp.bfloat16)
        pooled = jnp.dot(split, pooling, preferred_element_type=jnp.float32)
        means = pooled[: sums.shape[0]] + pooled[sums.shape[0] :]
        power_other = means[:looks]
        powers[place] = power_other
        for k in range(1, mates + 1):
            mean_real = means[(2 * k - 1) * looks : 2 * k * looks]
            mean_imag = means[2 * k * looks : (2 * k + 1) * looks]
            power_own = powers[(date + window - k) % window]
            scale = 1.0 / jnp.sqrt(power_own * power_other + EPSILON)
            amplitude = jnp.sqrt(mean_real * mean_real + mean_imag * mean_imag) * scale

            @pl.when(date >= k)
            def _():
                flag = flags_scalar[k - 1, date - k].astype(jnp.float32)
                shown = amplitude * flag
                if k > 1:
                    shown = coh[date - k] + pltpu.roll(shown, (k - 1) * looked_cols, 1)
                coh[date - k] = shown
                phases[(date - k) * mates + (k - 1)] = mean_imag * scale

        @pl.when(date >= mates)
        def _():
            hand_out(date - mates)

        return carry

    lax.fori_loop(0, dates, one_date, 0)
    lax.fori_loop(dates - mates, dates, lambda date, carry: (hand_out(date), carry)[1], 0)

    listed = targets[pl.ds(me, 1), :]
    diagonal = iota((slots, slots), 0) == iota((slots, slots), 1)
    row_of = (listed // looked_cols).astype(jnp.float32)
    column_of = (listed % looked_cols).astype(jnp.float32)
    row_down = jnp.sum(jnp.where(diagonal, row_of, 0.0), axis=1, keepdims=True)
    column_down = jnp.sum(jnp.where(diagonal, column_of, 0.0), axis=1, keepdims=True)
    by_column = jnp.where(
        iota((slots, LANES), 1).astype(jnp.float32) == column_down, 1.0, 0.0
    )
    flat_phases = phases[...].reshape(pairs * looks, LANES)
    rows_picked = lax.dot_general(
        by_column,
        flat_phases,
        (((1,), (1,)), ((), ())),
        precision=HIGHEST,
        preferred_element_type=jnp.float32,
    )
    lane = iota((slots, pairs * looks), 1)
    picked = jnp.where((lane % looks).astype(jnp.float32) == row_down, rows_picked, 0.0)
    expand = jnp.where(
        iota((mapping.shape[1], pairs * looks), 1) // looks
        == iota((mapping.shape[1], pairs * looks), 0),
        1.0,
        0.0,
    )
    wide = jnp.dot(mapping, expand, precision=HIGHEST, preferred_element_type=jnp.float32)
    result = lax.dot_general(
        wide,
        picked,
        (((1,), (1,)), ((), ())),
        precision=HIGHEST,
        preferred_element_type=jnp.float32,
    )
    result = jnp.where(iota(result.shape, 1) < totals[me], result, 0.0)
    velocities[...] = result[: dates - 1]

    own_coh.wait()

    def finish(step, carry):
        other = (me + step) % dates
        image_copy(other, me).wait_send()
        coh_copy(other, me).wait_send()
        coh_copy(other, other).wait_recv()
        return carry

    lax.fori_loop(1, dates, finish, 0)
    across_rows = jnp.transpose(gathered[...])
    for k in range(mates):
        coherence[0, k] = across_rows[k * looked_cols : (k + 1) * looked_cols]


def local(
    full_resolution_frames,
    height_angle_factor,
    normal_spacings,
    couple_entry_flags,
    block_target_indices,
    block_target_totals,
):
    dates, mates = couple_entry_flags.shape
    image_rows, cols = height_angle_factor.shape
    rows = image_rows // dates
    tiles = cols // LANES
    looks = rows // LOOK_ROWS
    looked_cols = cols // LOOK_COLS
    slots = block_target_indices.shape[1]
    window = mates + 1
    f32 = jnp.float32
    vmem = pl.BlockSpec(memory_space=pltpu.VMEM)
    smem = pl.BlockSpec(memory_space=pltpu.SMEM)
    hbm = pl.BlockSpec(memory_space=pltpu.HBM)
    coherence, velocities = pl.pallas_call(
        functools.partial(kernel, dates, mates),
        out_shape=(
            jax.ShapeDtypeStruct((1, mates, looked_cols, image_rows // LOOK_ROWS), f32),
            jax.ShapeDtypeStruct((dates - 1, slots), f32),
        ),
        in_specs=[hbm, hbm, smem, smem, vmem, vmem, smem],
        out_specs=(vmem, vmem),
        scratch_shapes=[
            pltpu.VMEM((dates, 2, rows, cols), jnp.bfloat16),
            pltpu.VMEM((rows, cols), f32),
            pltpu.VMEM((2, tiles, rows, LANES), f32),
            pltpu.VMEM((LOOK_ROWS, tiles, looks, LANES), f32),
            pltpu.VMEM((window, 2, LOOK_ROWS, tiles, looks, LANES), f32),
            pltpu.VMEM((window, looks, LANES), f32),
            pltpu.VMEM((dates * mates, looks, LANES), f32),
            pltpu.VMEM((dates, looks, LANES), f32),
            pltpu.VMEM((image_rows // LOOK_ROWS, LANES), f32),
            pltpu.SemaphoreType.DMA((dates,)),
            pltpu.SemaphoreType.DMA((dates,)),
            pltpu.SemaphoreType.DMA((dates,)),
            pltpu.SemaphoreType.DMA((dates,)),
            pltpu.SemaphoreType.DMA((3,)),
        ],
        compiler_params=pltpu.CompilerParams(
            collective_id=0, has_side_effects=True, vmem_limit_bytes=62 * 1024 * 1024
        ),
    )(
        full_resolution_frames,
        height_angle_factor,
        normal_spacings,
        couple_entry_flags.T,
        couple_entry_flags.T,
        block_target_indices,
        block_target_totals,
    )
    return jnp.swapaxes(coherence, 2, 3), velocities.T


def solution(mesh):
    in_specs = (
        P(("grp", "tile"), None, None, None),
        P("grp", None),
        P("grp"),
        P(),
        P("grp", None),
        P("grp"),
    )
    out_specs = (P(("grp", "tile"), None, None, None), P(("grp", "tile"), None))
    return jax.shard_map(local, mesh=mesh, in_specs=in_specs, out_specs=out_specs, check_vma=False)
```

```python
import functools

import jax
import jax.numpy as jnp
from jax import lax
from jax.experimental import pallas as pl
from jax.experimental.pallas import tpu as pltpu
from jax.sharding import PartitionSpec as P

LOOK_ROWS = 4
LOOK_COLS = 16
LANES = 128
EPSILON = 1e-06
HIGHEST = lax.Precision.HIGHEST


def iota(shape, axis):
    return lax.broadcasted_iota(jnp.int32, shape, axis)


def sine_cosine(x):
    turns = jnp.round(x * 0.6366197723675814)
    r = (x - turns * 1.5703125) - turns * 4.838267948966e-4
    z = r * r
    s = r + r * z * (-1.6666654611e-1 + z * (8.3321608736e-3 + z * -1.9515295891e-4))
    c = 1.0 - 0.5 * z + z * z * (
        4.166664568298827e-2 + z * (-1.388731625493765e-3 + z * 2.443315711809948e-5)
    )
    quarter = turns.astype(jnp.int32)
    odd = (quarter & 1) == 1
    sine = jnp.where(odd, c, s) * (1 - (quarter & 2)).astype(jnp.float32)
    cosine = jnp.where(odd, s, c) * (1 - ((quarter + 1) & 2)).astype(jnp.float32)
    return sine, cosine


def inverse_map(flags, dates, mates):
    intervals = dates - 1
    rows = -(-intervals // 8) * 8
    pairs = -(-dates * mates // LANES) * LANES
    own_slot = iota((dates, pairs), 1) // mates == iota((dates, pairs), 0)
    spread = jnp.dot(
        flags.astype(jnp.bfloat16),
        jnp.where(own_slot, 1.0, 0.0).astype(jnp.bfloat16),
        preferred_element_type=jnp.float32,
    )
    kind = iota((mates, pairs), 1) % mates == iota((mates, pairs), 0)
    used = jnp.sum(jnp.where(kind, spread, 0.0), axis=0, keepdims=True)
    interval = iota((rows, pairs), 0)
    pair = iota((rows, pairs), 1)
    first = pair // mates
    covered = (interval >= first) & (interval < first + pair % mates + 1) & (interval < intervals)
    right = jnp.where(covered, used, 0.0)
    normal = lax.dot_general(
        right.astype(jnp.bfloat16),
        right.astype(jnp.bfloat16),
        (((1,), (1,)), ((), ())),
        preferred_element_type=jnp.float32,
    )
    down = iota((rows, rows), 0)
    across = iota((rows, rows), 1)
    down_right = iota((rows, pairs), 0)

    def eliminate(t, carry):
        a, b = carry
        row_a = jnp.sum(jnp.where(down == t, a, 0.0), axis=0, keepdims=True)
        row_b = jnp.sum(jnp.where(down_right == t, b, 0.0), axis=0, keepdims=True)
        column = jnp.sum(jnp.where(across == t, a, 0.0), axis=1, keepdims=True)
        pivot = jnp.sum(jnp.where(across[:1] == t, row_a, 0.0), axis=1, keepdims=True)
        row_a = row_a / pivot
        row_b = row_b / pivot
        return (
            jnp.where(down == t, row_a, a - column * row_a),
            jnp.where(down_right == t, row_b, b - column * row_b),
        )

    return lax.fori_loop(0, intervals, eliminate, (normal, right))[1]


def kernel(
    dates,
    mates,
    group,
    frames,
    heights,
    spacings,
    flags_scalar,
    flags_vector,
    targets,
    totals,
    coherence,
    velocities,
    held,
    height_rows,
    natural,
    height_looks,
    rotated,
    powers,
    phases,
    coh,
    gathered,
    gathered_late,
    partial,
    partials,
    send_sem,
    recv_sem,
    coh_send_sem,
    coh_recv_sem,
    late_send_sem,
    late_recv_sem,
    part_send_sem,
    part_recv_sem,
    local_sem,
):
    me = lax.axis_index("tile")
    g = me // group
    q = me % group
    groups = dates // group
    share = dates // group
    half = share // 2
    cols = held.shape[3]
    rows = held.shape[2] // share
    tiles = cols // LANES
    looks = rows // LOOK_ROWS
    looked_cols = cols // LOOK_COLS
    slots = targets.shape[1]
    window = rotated.shape[0]
    base = g * group - mates
    own_slot = q + mates

    def share_rows(member, first, count, unit):
        return pl.ds(pl.multiple_of((member * share + first) * unit, unit), count * unit)

    own_block = pltpu.make_async_copy(
        frames.at[0, :, share_rows(q, 0, share, rows), :], held.at[own_slot], local_sem.at[0]
    )
    own_heights = pltpu.make_async_copy(
        heights.at[share_rows(q, 0, share, rows), :], height_rows, local_sem.at[1]
    )
    own_block.start()
    own_heights.start()
    gathered_late[...] = jnp.zeros_like(gathered_late)

    barrier = pltpu.get_barrier_semaphore()

    def greet(step, carry):
        pl.semaphore_signal(
            barrier,
            inc=1,
            device_id={"tile": (me + step) % dates},
            device_id_type=pl.DeviceIdType.MESH,
        )
        return carry

    lax.fori_loop(1, dates, greet, 0)
    pl.semaphore_wait(barrier, dates - 1)

    def remote(src, dst, send, recv, to):
        return pltpu.make_async_remote_copy(
            src_ref=src,
            dst_ref=dst,
            send_sem=send,
            recv_sem=recv,
            device_id={"tile": to},
            device_id_type=pl.DeviceIdType.MESH,
        )

    def image_copy(member, slot):
        return remote(
            frames.at[0, :, share_rows(member, 0, share, rows), :],
            held.at[slot],
            send_sem.at[1, member],
            recv_sem.at[slot],
            g * group + member,
        )

    def to_previous(member):
        return remote(
            frames.at[0, :, share_rows(member, 0, half, rows), :],
            held.at[q + group + mates, :, pl.ds(0, half * rows), :],
            send_sem.at[0, member],
            recv_sem.at[q + group + mates],
            (g - 1) * group + member,
        )

    def to_next(member):
        return remote(
            frames.at[0, :, share_rows(member, half, share - half, rows), :],
            held.at[q - group + mates, :, pl.ds(half * rows, (share - half) * rows), :],
            send_sem.at[2, member],
            recv_sem.at[q - group + mates],
            (g + 1) * group + member,
        )

    def from_next(slot):
        place = held.at[slot, :, pl.ds(0, half * rows), :]
        return remote(place, place, send_sem.at[0, 0], recv_sem.at[slot], (me + 1) % dates)

    def from_previous(slot):
        place = held.at[slot, :, pl.ds(half * rows, (share - half) * rows), :]
        return remote(place, place, send_sem.at[0, 0], recv_sem.at[slot], (me + 1) % dates)

    feeds_previous = (g > 0) & (q < mates)
    feeds_next = (g < groups - 1) & (q >= group - mates)

    def partner(step):
        return q ^ step if group & (group - 1) == 0 else (q + step) % group

    def send_beyond(member, carry):
        @pl.when(feeds_previous)
        def _():
            to_previous(member).start()

        @pl.when(feeds_next)
        def _():
            to_next(member).start()

        return carry

    def send_image(step, carry):
        image_copy(partner(group - step), own_slot).start()
        return carry

    lax.fori_loop(0, group, send_beyond, 0)
    lax.fori_loop(1, group, send_image, 0)

    rotated[...] = jnp.zeros_like(rotated)
    powers[...] = jnp.zeros_like(powers)
    phases[...] = jnp.zeros_like(phases)
    coh[...] = jnp.zeros_like(coh)
    assert mates * looked_cols <= LANES

    mapping = inverse_map(flags_vector[...], dates, mates)

    look_lane = iota((cols, LANES), 1)
    pooling = jnp.where(
        iota((cols, LANES), 0) // LOOK_COLS == look_lane, 1.0 / (LOOK_ROWS * LOOK_COLS), 0.0
    ).astype(jnp.bfloat16)

    own_block.wait()
    own_heights.wait()

    def one_tile(tile, carry):
        lower = tile // half
        tile_rows = pl.ds(pl.multiple_of(tile * rows, rows), rows)
        tile_looks = pl.ds(pl.multiple_of(tile * looks, looks), looks)
        for c in range(tiles):
            natural[0, c] = height_rows[tile_rows, c * LANES : (c + 1) * LANES]
        for j in range(LOOK_ROWS):
            height_looks[j] = natural[0, :, pl.ds(j, looks, stride=LOOK_ROWS), :]

        def one_date(step, carry):
            slot = step + mates * (1 - lower)
            date = base + slot

            @pl.when((date >= 0) & (date < dates))
            def _():
                visit(step, slot, date)

            return carry

        def visit(step, slot, date):
            @pl.when((tile == 0) & (slot < group + mates) & (slot != own_slot))
            def _():
                image_copy(slot - mates, slot).wait_recv()

            @pl.when((tile == 0) & (slot >= group + mates))
            def _():
                from_next(slot).wait_recv()

            @pl.when((tile == half) & (slot < mates))
            def _():
                from_previous(slot).wait_recv()

            place = slot % window
            for plane in range(2):
                for c in range(tiles):
                    natural[plane, c] = held[
                        slot, plane, tile_rows, c * LANES : (c + 1) * LANES
                    ].astype(jnp.float32)
            spacing = spacings[date]
            power = None
            for j in range(LOOK_ROWS):
                real = natural[0, :, pl.ds(j, looks, stride=LOOK_ROWS), :]
                imag = natural[1, :, pl.ds(j, looks, stride=LOOK_ROWS), :]
                sine, cosine = sine_cosine(spacing * height_looks[j])
                rotated[place, 0, j] = real * cosine + imag * sine
                rotated[place, 1, j] = imag * cosine - real * sine
                energy = real * real + imag * imag
                power = energy if j == 0 else power + energy
            fields = [power]
            for k in range(1, mates + 1):
                other = (slot + window - k) % window
                flat_real = 0.0
                flat_imag = 0.0
                for j in range(LOOK_ROWS):
                    a_real = rotated[other, 0, j]
                    a_imag = rotated[other, 1, j]
                    c_real = rotated[place, 0, j]
                    c_imag = rotated[place, 1, j]
                    flat_real = flat_real + (a_real * c_real + a_imag * c_imag)
                    flat_imag = flat_imag + (a_imag * c_real - a_real * c_imag)
                fields += [flat_real, flat_imag]
            sums = jnp.concatenate(
                [jnp.concatenate([field[c] for c in range(tiles)], axis=1) for field in fields],
                axis=0,
            )
            high = sums.astype(jnp.bfloat16).astype(jnp.float32)
            split = jnp.concatenate([high, sums - high], axis=0).astype(jnp.bfloat16)
            pooled = jnp.dot(split, pooling, preferred_element_type=jnp.float32)
            means = pooled[: sums.shape[0]] + pooled[sums.shape[0] :]
            power_other = means[:looks]
            powers[place] = power_other
            for k in range(1, mates + 1):
                mean_real = means[(2 * k - 1) * looks : 2 * k * looks]
                mean_imag = means[2 * k * looks : (2 * k + 1) * looks]
                power_own = powers[(slot + window - k) % window]
                scale = 1.0 / jnp.sqrt(power_own * power_other + EPSILON)
                amplitude = jnp.sqrt(mean_real * mean_real + mean_imag * mean_imag) * scale

                @pl.when((step >= k) & (date >= k) & (slot >= mates) & (slot - k < group + mates))
                def _():
                    flag = flags_scalar[k - 1, date - k].astype(jnp.float32)
                    shown = amplitude * flag
                    if k > 1:
                        shown = pltpu.roll(shown, (k - 1) * looked_cols, 1)
                    coh[slot - k, tile_looks, :] = coh[slot - k, tile_looks, :] + shown
                    phases[tile, (slot - k) * mates + (k - 1)] = mean_imag * scale

        lax.fori_loop(0, group + mates, one_date, 0)
        return carry

    lax.fori_loop(0, share, one_tile, 0)

    def coh_copy(to, member):
        return remote(
            coh.at[to + mates],
            gathered.at[share_rows(member, 0, share, looks), :],
            coh_send_sem.at[to],
            coh_recv_sem.at[member],
            g * group + to,
        )

    def late_copy(slot, member):
        return remote(
            coh.at[slot, pl.ds(half * looks, (share - half) * looks), :],
            gathered_late.at[share_rows(member, half, share - half, looks), :],
            late_send_sem.at[slot],
            late_recv_sem.at[member],
            (base + slot + dates) % dates,
        )

    own_coh = pltpu.make_async_copy(
        coh.at[own_slot], gathered.at[share_rows(q, 0, share, looks), :], local_sem.at[2]
    )
    own_coh.start()
    lax.fori_loop(
        1, group, lambda step, carry: (coh_copy(partner(group - step), q).start(), carry)[1], 0
    )

    @pl.when(g > 0)
    def _():
        lax.fori_loop(0, mates, lambda slot, carry: (late_copy(slot, q).start(), carry)[1], 0)

    kept = phases.shape[1]
    offset = base * mates
    expand = jnp.where(
        iota((mapping.shape[1], kept * looks), 1) // looks + offset
        == iota((mapping.shape[1], kept * looks), 0),
        1.0,
        0.0,
    )
    wide = jnp.dot(mapping, expand, precision=HIGHEST, preferred_element_type=jnp.float32)

    def part_copy(tile, source, to):
        return remote(
            partial.at[tile],
            partials.at[source],
            part_send_sem.at[tile],
            part_recv_sem.at[source],
            to,
        )

    def own_part(tile):
        return pltpu.make_async_copy(partial.at[tile], partials.at[g], local_sem.at[3])

    def pick(tile, carry):
        whole_tile = q * share + tile
        listed = targets[pl.ds(whole_tile, 1), :]
        diagonal = iota((slots, slots), 0) == iota((slots, slots), 1)
        row_of = (listed // looked_cols).astype(jnp.float32)
        column_of = (listed % looked_cols).astype(jnp.float32)
        row_down = jnp.sum(jnp.where(diagonal, row_of, 0.0), axis=1, keepdims=True)
        column_down = jnp.sum(jnp.where(diagonal, column_of, 0.0), axis=1, keepdims=True)
        by_column = jnp.where(
            iota((slots, LANES), 1).astype(jnp.float32) == column_down, 1.0, 0.0
        )
        flat_phases = phases[tile].reshape(kept * looks, LANES)
        rows_picked = lax.dot_general(
            by_column,
            flat_phases,
            (((1,), (1,)), ((), ())),
            precision=HIGHEST,
            preferred_element_type=jnp.float32,
        )
        lane = iota((slots, kept * looks), 1)
        picked = jnp.where((lane % looks).astype(jnp.float32) == row_down, rows_picked, 0.0)
        result = lax.dot_general(
            wide,
            picked,
            (((1,), (1,)), ((), ())),
            precision=HIGHEST,
            preferred_element_type=jnp.float32,
        )
        partial[tile] = jnp.where(iota(result.shape, 1) < totals[whole_tile], result, 0.0)

        @pl.when(whole_tile == me)
        def _():
            own_part(tile).start()

        @pl.when(whole_tile != me)
        def _():
            part_copy(tile, g, whole_tile).start()

        return carry

    lax.fori_loop(0, share, pick, 0)

    own_coh.wait()

    def finish(step, carry):
        other = (q + step) % group
        image_copy(other, own_slot).wait_send()
        coh_copy(other, q).wait_send()
        coh_copy(other, other).wait_recv()
        return carry

    lax.fori_loop(1, group, finish, 0)

    def finish_beyond(member, carry):
        @pl.when(feeds_previous)
        def _():
            to_previous(member).wait_send()

        @pl.when(feeds_next)
        def _():
            to_next(member).wait_send()
            late_copy(0, member).wait_recv()

        return carry

    lax.fori_loop(0, group, finish_beyond, 0)

    @pl.when(g > 0)
    def _():
        lax.fori_loop(0, mates, lambda slot, carry: (late_copy(slot, q).wait_send(), carry)[1], 0)

    across_rows = jnp.transpose(gathered[...] + gathered_late[...])
    for k in range(mates):
        coherence[0, k] = across_rows[k * looked_cols : (k + 1) * looked_cols]

    def finish_part(tile, carry):
        whole_tile = q * share + tile

        @pl.when(whole_tile == me)
        def _():
            own_part(tile).wait()

        @pl.when(whole_tile != me)
        def _():
            part_copy(tile, g, whole_tile).wait_send()

        return carry

    lax.fori_loop(0, share, finish_part, 0)

    def arrive(source, carry):
        @pl.when(source * group + me // share != me)
        def _():
            part_copy(0, source, (me + 1) % dates).wait_recv()

        return carry

    lax.fori_loop(0, groups, arrive, 0)
    velocities[...] = jnp.sum(partials[...], axis=0)[: dates - 1]


def local(
    full_resolution_frames,
    height_angle_factor,
    normal_spacings,
    couple_entry_flags,
    block_target_indices,
    block_target_totals,
):
    dates, mates = couple_entry_flags.shape
    image_rows, cols = height_angle_factor.shape
    group = 8
    share = dates // group
    assert dates % group == 0 and share % 2 == 0
    rows = image_rows // dates
    tiles = cols // LANES
    looks = rows // LOOK_ROWS
    looked_cols = cols // LOOK_COLS
    slots = block_target_indices.shape[1]
    window = mates + 1
    padded = -(-(dates - 1) // 8) * 8
    f32 = jnp.float32
    vmem = pl.BlockSpec(memory_space=pltpu.VMEM)
    smem = pl.BlockSpec(memory_space=pltpu.SMEM)
    hbm = pl.BlockSpec(memory_space=pltpu.HBM)
    coherence, velocities = pl.pallas_call(
        functools.partial(kernel, dates, mates, group),
        out_shape=(
            jax.ShapeDtypeStruct((1, mates, looked_cols, image_rows // LOOK_ROWS), f32),
            jax.ShapeDtypeStruct((dates - 1, slots), f32),
        ),
        in_specs=[hbm, hbm, smem, smem, vmem, vmem, smem],
        out_specs=(vmem, vmem),
        scratch_shapes=[
            pltpu.VMEM((group + 2 * mates, 2, share * rows, cols), jnp.bfloat16),
            pltpu.VMEM((share * rows, cols), f32),
            pltpu.VMEM((2, tiles, rows, LANES), f32),
            pltpu.VMEM((LOOK_ROWS, tiles, looks, LANES), f32),
            pltpu.VMEM((window, 2, LOOK_ROWS, tiles, looks, LANES), f32),
            pltpu.VMEM((window, looks, LANES), f32),
            pltpu.VMEM((share, (group + mates) * mates, looks, LANES), f32),
            pltpu.VMEM((group + mates, share * looks, LANES), f32),
            pltpu.VMEM((image_rows // LOOK_ROWS, LANES), f32),
            pltpu.VMEM((image_rows // LOOK_ROWS, LANES), f32),
            pltpu.VMEM((share, padded, slots), f32),
            pltpu.VMEM((dates // group, padded, slots), f32),
            pltpu.SemaphoreType.DMA((3, group)),
            pltpu.SemaphoreType.DMA((group + 2 * mates,)),
            pltpu.SemaphoreType.DMA((group,)),
            pltpu.SemaphoreType.DMA((group,)),
            pltpu.SemaphoreType.DMA((mates,)),
            pltpu.SemaphoreType.DMA((group,)),
            pltpu.SemaphoreType.DMA((share,)),
            pltpu.SemaphoreType.DMA((dates // group,)),
            pltpu.SemaphoreType.DMA((4,)),
        ],
        compiler_params=pltpu.CompilerParams(
            collective_id=0, has_side_effects=True, vmem_limit_bytes=62 * 1024 * 1024
        ),
    )(
        full_resolution_frames,
        height_angle_factor,
        normal_spacings,
        couple_entry_flags.T,
        couple_entry_flags.T,
        block_target_indices,
        block_target_totals,
    )
    return jnp.swapaxes(coherence, 2, 3), velocities.T


def solution(mesh):
    in_specs = (
        P(("grp", "tile"), None, None, None),
        P("grp", None),
        P("grp"),
        P(),
        P("grp", None),
        P("grp"),
    )
    out_specs = (P(("grp", "tile"), None, None, None), P(("grp", "tile"), None))
    return jax.shard_map(local, mesh=mesh, in_specs=in_specs, out_specs=out_specs, check_vma=False)
```

```python
import functools

import jax
import jax.numpy as jnp
from jax import lax
from jax.experimental import pallas as pl
from jax.experimental.pallas import tpu as pltpu
from jax.sharding import PartitionSpec as P

LOOK_ROWS = 4
LOOK_COLS = 16
LANES = 128
EPSILON = 1e-06
HIGHEST = lax.Precision.HIGHEST


def iota(shape, axis):
    return lax.broadcasted_iota(jnp.int32, shape, axis)


def sine_cosine(x):
    turns = jnp.round(x * 0.6366197723675814)
    r = (x - turns * 1.5703125) - turns * 4.838267948966e-4
    z = r * r
    s = r + r * z * (-1.6666654611e-1 + z * (8.3321608736e-3 + z * -1.9515295891e-4))
    c = 1.0 - 0.5 * z + z * z * (
        4.166664568298827e-2 + z * (-1.388731625493765e-3 + z * 2.443315711809948e-5)
    )
    quarter = turns.astype(jnp.int32)
    odd = (quarter & 1) == 1
    sine = jnp.where(odd, c, s) * (1 - (quarter & 2)).astype(jnp.float32)
    cosine = jnp.where(odd, s, c) * (1 - ((quarter + 1) & 2)).astype(jnp.float32)
    return sine, cosine


def inverse_map(flags, dates, mates):
    intervals = dates - 1
    rows = -(-intervals // 8) * 8
    pairs = -(-dates * mates // LANES) * LANES
    own_slot = iota((dates, pairs), 1) // mates == iota((dates, pairs), 0)
    spread = jnp.dot(
        flags.astype(jnp.bfloat16),
        jnp.where(own_slot, 1.0, 0.0).astype(jnp.bfloat16),
        preferred_element_type=jnp.float32,
    )
    kind = iota((mates, pairs), 1) % mates == iota((mates, pairs), 0)
    used = jnp.sum(jnp.where(kind, spread, 0.0), axis=0, keepdims=True)
    interval = iota((rows, pairs), 0)
    pair = iota((rows, pairs), 1)
    first = pair // mates
    covered = (interval >= first) & (interval < first + pair % mates + 1) & (interval < intervals)
    right = jnp.where(covered, used, 0.0)
    normal = lax.dot_general(
        right.astype(jnp.bfloat16),
        right.astype(jnp.bfloat16),
        (((1,), (1,)), ((), ())),
        preferred_element_type=jnp.float32,
    )
    down = iota((rows, rows), 0)
    across = iota((rows, rows), 1)
    down_right = iota((rows, pairs), 0)

    def eliminate(t, carry):
        a, b = carry
        row_a = jnp.sum(jnp.where(down == t, a, 0.0), axis=0, keepdims=True)
        row_b = jnp.sum(jnp.where(down_right == t, b, 0.0), axis=0, keepdims=True)
        column = jnp.sum(jnp.where(across == t, a, 0.0), axis=1, keepdims=True)
        pivot = jnp.sum(jnp.where(across[:1] == t, row_a, 0.0), axis=1, keepdims=True)
        row_a = row_a / pivot
        row_b = row_b / pivot
        return (
            jnp.where(down == t, row_a, a - column * row_a),
            jnp.where(down_right == t, row_b, b - column * row_b),
        )

    return lax.fori_loop(0, intervals, eliminate, (normal, right))[1]


def kernel(
    dates,
    mates,
    group,
    frames,
    heights,
    spacings,
    flags_scalar,
    flags_vector,
    targets,
    totals,
    coherence,
    velocities,
    held,
    height_rows,
    natural,
    height_looks,
    rotated,
    powers,
    phases,
    coh,
    gathered,
    gathered_late,
    partial,
    partials,
    send_sem,
    recv_sem,
    coh_send_sem,
    coh_recv_sem,
    late_send_sem,
    late_recv_sem,
    part_send_sem,
    part_recv_sem,
    local_sem,
):
    me = lax.axis_index("tile")
    g = me // group
    q = me % group
    groups = dates // group
    share = dates // group
    half = share // 2
    cols = held.shape[3]
    rows = held.shape[2] // share
    tiles = cols // LANES
    looks = rows // LOOK_ROWS
    looked_cols = cols // LOOK_COLS
    slots = targets.shape[1]
    window = rotated.shape[0]
    base = g * group - mates
    own_slot = q + mates

    def share_rows(member, first, count, unit):
        return pl.ds(pl.multiple_of((member * share + first) * unit, unit), count * unit)

    own_block = pltpu.make_async_copy(
        frames.at[0, :, share_rows(q, 0, share, rows), :], held.at[own_slot], local_sem.at[0]
    )
    own_heights = pltpu.make_async_copy(
        heights.at[share_rows(q, 0, share, rows), :], height_rows, local_sem.at[1]
    )
    own_block.start()
    own_heights.start()
    gathered_late[...] = jnp.zeros_like(gathered_late)

    barrier = pltpu.get_barrier_semaphore()

    def greet(step, carry):
        pl.semaphore_signal(
            barrier,
            inc=1,
            device_id={"tile": (me + step) % dates},
            device_id_type=pl.DeviceIdType.MESH,
        )
        return carry

    lax.fori_loop(1, dates, greet, 0)
    pl.semaphore_wait(barrier, dates - 1)

    def remote(src, dst, send, recv, to):
        return pltpu.make_async_remote_copy(
            src_ref=src,
            dst_ref=dst,
            send_sem=send,
            recv_sem=recv,
            device_id={"tile": to},
            device_id_type=pl.DeviceIdType.MESH,
        )

    def image_copy(member, slot, part):
        return remote(
            frames.at[0, :, share_rows(member, part * half, half, rows), :],
            held.at[slot, :, pl.ds(part * half * rows, half * rows), :],
            send_sem.at[1 + part, member],
            recv_sem.at[part, slot],
            g * group + member,
        )

    def to_previous(member):
        return remote(
            frames.at[0, :, share_rows(member, 0, half, rows), :],
            held.at[q + group + mates, :, pl.ds(0, half * rows), :],
            send_sem.at[0, member],
            recv_sem.at[0, q + group + mates],
            (g - 1) * group + member,
        )

    def to_next(member):
        return remote(
            frames.at[0, :, share_rows(member, half, share - half, rows), :],
            held.at[q - group + mates, :, pl.ds(half * rows, (share - half) * rows), :],
            send_sem.at[3, member],
            recv_sem.at[1, q - group + mates],
            (g + 1) * group + member,
        )

    def arrival(slot, part):
        place = held.at[slot, :, pl.ds(part * half * rows, half * rows), :]
        return remote(place, place, send_sem.at[0, 0], recv_sem.at[part, slot], (me + 1) % dates)

    feeds_previous = (g > 0) & (q < mates)
    feeds_next = (g < groups - 1) & (q >= group - mates)

    def partner(step):
        return q ^ step if group & (group - 1) == 0 else (q + step) % group

    @pl.when(feeds_previous)
    def _():
        lax.fori_loop(0, group, lambda member, carry: (to_previous(member).start(), carry)[1], 0)

    lax.fori_loop(
        1,
        group,
        lambda step, carry: (image_copy(partner(group - step), own_slot, 0).start(), carry)[1],
        0,
    )

    @pl.when(feeds_next)
    def _():
        lax.fori_loop(0, group, lambda member, carry: (to_next(member).start(), carry)[1], 0)

    lax.fori_loop(
        1,
        group,
        lambda step, carry: (image_copy(partner(group - step), own_slot, 1).start(), carry)[1],
        0,
    )

    rotated[...] = jnp.zeros_like(rotated)
    powers[...] = jnp.zeros_like(powers)
    phases[...] = jnp.zeros_like(phases)
    coh[...] = jnp.zeros_like(coh)
    assert mates * looked_cols <= LANES

    mapping = inverse_map(flags_vector[...], dates, mates)

    look_lane = iota((cols, LANES), 1)
    pooling = jnp.where(
        iota((cols, LANES), 0) // LOOK_COLS == look_lane, 1.0 / (LOOK_ROWS * LOOK_COLS), 0.0
    ).astype(jnp.bfloat16)

    kept = phases.shape[1]
    offset = base * mates
    expand = jnp.where(
        iota((mapping.shape[1], kept * looks), 1) // looks + offset
        == iota((mapping.shape[1], kept * looks), 0),
        1.0,
        0.0,
    )
    wide = jnp.dot(mapping, expand, precision=HIGHEST, preferred_element_type=jnp.float32)

    def part_copy(tile, source, to):
        return remote(
            partial.at[tile],
            partials.at[source],
            part_send_sem.at[tile],
            part_recv_sem.at[source],
            to,
        )

    def own_part(tile):
        return pltpu.make_async_copy(partial.at[tile], partials.at[g], local_sem.at[3])

    def pick(tile):
        whole_tile = q * share + tile
        listed = targets[pl.ds(whole_tile, 1), :]
        diagonal = iota((slots, slots), 0) == iota((slots, slots), 1)
        row_of = (listed // looked_cols).astype(jnp.float32)
        column_of = (listed % looked_cols).astype(jnp.float32)
        row_down = jnp.sum(jnp.where(diagonal, row_of, 0.0), axis=1, keepdims=True)
        column_down = jnp.sum(jnp.where(diagonal, column_of, 0.0), axis=1, keepdims=True)
        by_column = jnp.where(
            iota((slots, LANES), 1).astype(jnp.float32) == column_down, 1.0, 0.0
        )
        flat_phases = phases[tile].reshape(kept * looks, LANES)
        rows_picked = lax.dot_general(
            by_column,
            flat_phases,
            (((1,), (1,)), ((), ())),
            precision=HIGHEST,
            preferred_element_type=jnp.float32,
        )
        lane = iota((slots, kept * looks), 1)
        picked = jnp.where((lane % looks).astype(jnp.float32) == row_down, rows_picked, 0.0)
        result = lax.dot_general(
            wide,
            picked,
            (((1,), (1,)), ((), ())),
            precision=HIGHEST,
            preferred_element_type=jnp.float32,
        )
        partial[tile] = jnp.where(iota(result.shape, 1) < totals[whole_tile], result, 0.0)

        @pl.when(whole_tile == me)
        def _():
            own_part(tile).start()

        @pl.when(whole_tile != me)
        def _():
            part_copy(tile, g, whole_tile).start()

    own_block.wait()
    own_heights.wait()

    def one_tile(tile, carry):
        lower = tile // half
        tile_rows = pl.ds(pl.multiple_of(tile * rows, rows), rows)
        tile_looks = pl.ds(pl.multiple_of(tile * looks, looks), looks)
        for c in range(tiles):
            natural[0, c] = height_rows[tile_rows, c * LANES : (c + 1) * LANES]
        for j in range(LOOK_ROWS):
            height_looks[j] = natural[0, :, pl.ds(j, looks, stride=LOOK_ROWS), :]

        def one_date(step, carry):
            slot = step + mates * (1 - lower)
            date = base + slot

            @pl.when((date >= 0) & (date < dates))
            def _():
                visit(step, slot, date)

            return carry

        def visit(step, slot, date):
            @pl.when((tile == 0) & (slot != own_slot))
            def _():
                arrival(slot, 0).wait_recv()

            @pl.when((tile == half) & (slot != own_slot))
            def _():
                arrival(slot, 1).wait_recv()

            place = slot % window
            for plane in range(2):
                for c in range(tiles):
                    natural[plane, c] = held[
                        slot, plane, tile_rows, c * LANES : (c + 1) * LANES
                    ].astype(jnp.float32)
            spacing = spacings[date]
            power = None
            for j in range(LOOK_ROWS):
                real = natural[0, :, pl.ds(j, looks, stride=LOOK_ROWS), :]
                imag = natural[1, :, pl.ds(j, looks, stride=LOOK_ROWS), :]
                sine, cosine = sine_cosine(spacing * height_looks[j])
                rotated[place, 0, j] = real * cosine + imag * sine
                rotated[place, 1, j] = imag * cosine - real * sine
                energy = real * real + imag * imag
                power = energy if j == 0 else power + energy
            fields = [power]
            for k in range(1, mates + 1):
                other = (slot + window - k) % window
                flat_real = 0.0
                flat_imag = 0.0
                for j in range(LOOK_ROWS):
                    a_real = rotated[other, 0, j]
                    a_imag = rotated[other, 1, j]
                    c_real = rotated[place, 0, j]
                    c_imag = rotated[place, 1, j]
                    flat_real = flat_real + (a_real * c_real + a_imag * c_imag)
                    flat_imag = flat_imag + (a_imag * c_real - a_real * c_imag)
                fields += [flat_real, flat_imag]
            sums = jnp.concatenate(
                [jnp.concatenate([field[c] for c in range(tiles)], axis=1) for field in fields],
                axis=0,
            )
            high = sums.astype(jnp.bfloat16).astype(jnp.float32)
            split = jnp.concatenate([high, sums - high], axis=0).astype(jnp.bfloat16)
            pooled = jnp.dot(split, pooling, preferred_element_type=jnp.float32)
            means = pooled[: sums.shape[0]] + pooled[sums.shape[0] :]
            power_other = means[:looks]
            powers[place] = power_other
            for k in range(1, mates + 1):
                mean_real = means[(2 * k - 1) * looks : 2 * k * looks]
                mean_imag = means[2 * k * looks : (2 * k + 1) * looks]
                power_own = powers[(slot + window - k) % window]
                scale = 1.0 / jnp.sqrt(power_own * power_other + EPSILON)
                amplitude = jnp.sqrt(mean_real * mean_real + mean_imag * mean_imag) * scale

                @pl.when((step >= k) & (date >= k) & (slot >= mates) & (slot - k < group + mates))
                def _():
                    flag = flags_scalar[k - 1, date - k].astype(jnp.float32)
                    shown = amplitude * flag
                    if k > 1:
                        shown = pltpu.roll(shown, (k - 1) * looked_cols, 1)
                    coh[slot - k, tile_looks, :] = coh[slot - k, tile_looks, :] + shown
                    phases[tile, (slot - k) * mates + (k - 1)] = mean_imag * scale

        lax.fori_loop(0, group + mates, one_date, 0)

        @pl.when(tile < share - 1)
        def _():
            pick(tile)

        return carry

    lax.fori_loop(0, share, one_tile, 0)

    def coh_copy(to, member):
        return remote(
            coh.at[to + mates],
            gathered.at[share_rows(member, 0, share, looks), :],
            coh_send_sem.at[to],
            coh_recv_sem.at[member],
            g * group + to,
        )

    def late_copy(slot, member):
        return remote(
            coh.at[slot, pl.ds(half * looks, (share - half) * looks), :],
            gathered_late.at[share_rows(member, half, share - half, looks), :],
            late_send_sem.at[slot],
            late_recv_sem.at[member],
            (base + slot + dates) % dates,
        )

    own_coh = pltpu.make_async_copy(
        coh.at[own_slot], gathered.at[share_rows(q, 0, share, looks), :], local_sem.at[2]
    )
    own_coh.start()
    lax.fori_loop(
        1, group, lambda step, carry: (coh_copy(partner(group - step), q).start(), carry)[1], 0
    )

    @pl.when(g > 0)
    def _():
        lax.fori_loop(0, mates, lambda slot, carry: (late_copy(slot, q).start(), carry)[1], 0)

    pick(share - 1)

    own_coh.wait()

    def finish(step, carry):
        other = (q + step) % group
        image_copy(other, own_slot, 0).wait_send()
        image_copy(other, own_slot, 1).wait_send()
        coh_copy(other, q).wait_send()
        coh_copy(other, other).wait_recv()
        return carry

    lax.fori_loop(1, group, finish, 0)

    def finish_beyond(member, carry):
        @pl.when(feeds_previous)
        def _():
            to_previous(member).wait_send()

        @pl.when(feeds_next)
        def _():
            to_next(member).wait_send()
            late_copy(0, member).wait_recv()

        return carry

    lax.fori_loop(0, group, finish_beyond, 0)

    @pl.when(g > 0)
    def _():
        lax.fori_loop(0, mates, lambda slot, carry: (late_copy(slot, q).wait_send(), carry)[1], 0)

    across_rows = jnp.transpose(gathered[...] + gathered_late[...])
    for k in range(mates):
        coherence[0, k] = across_rows[k * looked_cols : (k + 1) * looked_cols]

    def finish_part(tile, carry):
        whole_tile = q * share + tile

        @pl.when(whole_tile == me)
        def _():
            own_part(tile).wait()

        @pl.when(whole_tile != me)
        def _():
            part_copy(tile, g, whole_tile).wait_send()

        return carry

    lax.fori_loop(0, share, finish_part, 0)

    def arrive(source, carry):
        @pl.when(source * group + me // share != me)
        def _():
            part_copy(0, source, (me + 1) % dates).wait_recv()

        return carry

    lax.fori_loop(0, groups, arrive, 0)
    velocities[...] = jnp.sum(partials[...], axis=0)[: dates - 1]


def local(
    full_resolution_frames,
    height_angle_factor,
    normal_spacings,
    couple_entry_flags,
    block_target_indices,
    block_target_totals,
):
    dates, mates = couple_entry_flags.shape
    image_rows, cols = height_angle_factor.shape
    group = 8
    share = dates // group
    assert dates % group == 0 and share % 2 == 0
    rows = image_rows // dates
    tiles = cols // LANES
    looks = rows // LOOK_ROWS
    looked_cols = cols // LOOK_COLS
    slots = block_target_indices.shape[1]
    window = mates + 1
    padded = -(-(dates - 1) // 8) * 8
    f32 = jnp.float32
    vmem = pl.BlockSpec(memory_space=pltpu.VMEM)
    smem = pl.BlockSpec(memory_space=pltpu.SMEM)
    hbm = pl.BlockSpec(memory_space=pltpu.HBM)
    coherence, velocities = pl.pallas_call(
        functools.partial(kernel, dates, mates, group),
        out_shape=(
            jax.ShapeDtypeStruct((1, mates, looked_cols, image_rows // LOOK_ROWS), f32),
            jax.ShapeDtypeStruct((dates - 1, slots), f32),
        ),
        in_specs=[hbm, hbm, smem, smem, vmem, vmem, smem],
        out_specs=(vmem, vmem),
        scratch_shapes=[
            pltpu.VMEM((group + 2 * mates, 2, share * rows, cols), jnp.bfloat16),
            pltpu.VMEM((share * rows, cols), f32),
            pltpu.VMEM((2, tiles, rows, LANES), f32),
            pltpu.VMEM((LOOK_ROWS, tiles, looks, LANES), f32),
            pltpu.VMEM((window, 2, LOOK_ROWS, tiles, looks, LANES), f32),
            pltpu.VMEM((window, looks, LANES), f32),
            pltpu.VMEM((share, (group + mates) * mates, looks, LANES), f32),
            pltpu.VMEM((group + mates, share * looks, LANES), f32),
            pltpu.VMEM((image_rows // LOOK_ROWS, LANES), f32),
            pltpu.VMEM((image_rows // LOOK_ROWS, LANES), f32),
            pltpu.VMEM((share, padded, slots), f32),
            pltpu.VMEM((dates // group, padded, slots), f32),
            pltpu.SemaphoreType.DMA((4, group)),
            pltpu.SemaphoreType.DMA((2, group + 2 * mates)),
            pltpu.SemaphoreType.DMA((group,)),
            pltpu.SemaphoreType.DMA((group,)),
            pltpu.SemaphoreType.DMA((mates,)),
            pltpu.SemaphoreType.DMA((group,)),
            pltpu.SemaphoreType.DMA((share,)),
            pltpu.SemaphoreType.DMA((dates // group,)),
            pltpu.SemaphoreType.DMA((4,)),
        ],
        compiler_params=pltpu.CompilerParams(
            collective_id=0, has_side_effects=True, vmem_limit_bytes=62 * 1024 * 1024
        ),
    )(
        full_resolution_frames,
        height_angle_factor,
        normal_spacings,
        couple_entry_flags.T,
        couple_entry_flags.T,
        block_target_indices,
        block_target_totals,
    )
    return jnp.swapaxes(coherence, 2, 3), velocities.T


def solution(mesh):
    in_specs = (
        P(("grp", "tile"), None, None, None),
        P("grp", None),
        P("grp"),
        P(),
        P("grp", None),
        P("grp"),
    )
    out_specs = (P(("grp", "tile"), None, None, None), P(("grp", "tile"), None))
    return jax.shard_map(local, mesh=mesh, in_specs=in_specs, out_specs=out_specs, check_vma=False)
```

```python
import functools

import jax
import jax.numpy as jnp
from jax import lax
from jax.experimental import pallas as pl
from jax.experimental.pallas import tpu as pltpu
from jax.sharding import PartitionSpec as P

LOOK_ROWS = 4
LOOK_COLS = 16
LANES = 128
EPSILON = 1e-06
HIGHEST = lax.Precision.HIGHEST


def iota(shape, axis):
    return lax.broadcasted_iota(jnp.int32, shape, axis)


def sine_cosine(x):
    turns = jnp.round(x * 0.6366197723675814)
    r = (x - turns * 1.5703125) - turns * 4.838267948966e-4
    z = r * r
    s = r + r * z * (-1.6666654611e-1 + z * (8.3321608736e-3 + z * -1.9515295891e-4))
    c = 1.0 - 0.5 * z + z * z * (
        4.166664568298827e-2 + z * (-1.388731625493765e-3 + z * 2.443315711809948e-5)
    )
    quarter = turns.astype(jnp.int32)
    odd = (quarter & 1) == 1
    sine = jnp.where(odd, c, s) * (1 - (quarter & 2)).astype(jnp.float32)
    cosine = jnp.where(odd, s, c) * (1 - ((quarter + 1) & 2)).astype(jnp.float32)
    return sine, cosine


def inverse_map(flags, dates, mates):
    intervals = dates - 1
    rows = -(-intervals // 8) * 8
    pairs = -(-dates * mates // LANES) * LANES
    own_slot = iota((dates, pairs), 1) // mates == iota((dates, pairs), 0)
    spread = jnp.dot(
        flags.astype(jnp.bfloat16),
        jnp.where(own_slot, 1.0, 0.0).astype(jnp.bfloat16),
        preferred_element_type=jnp.float32,
    )
    kind = iota((mates, pairs), 1) % mates == iota((mates, pairs), 0)
    used = jnp.sum(jnp.where(kind, spread, 0.0), axis=0, keepdims=True)
    interval = iota((rows, pairs), 0)
    pair = iota((rows, pairs), 1)
    first = pair // mates
    covered = (interval >= first) & (interval < first + pair % mates + 1) & (interval < intervals)
    right = jnp.where(covered, used, 0.0)
    normal = lax.dot_general(
        right.astype(jnp.bfloat16),
        right.astype(jnp.bfloat16),
        (((1,), (1,)), ((), ())),
        preferred_element_type=jnp.float32,
    )
    down = iota((rows, rows), 0)
    across = iota((rows, rows), 1)
    down_right = iota((rows, pairs), 0)

    def eliminate(t, carry):
        a, b = carry
        row_a = jnp.sum(jnp.where(down == t, a, 0.0), axis=0, keepdims=True)
        row_b = jnp.sum(jnp.where(down_right == t, b, 0.0), axis=0, keepdims=True)
        column = jnp.sum(jnp.where(across == t, a, 0.0), axis=1, keepdims=True)
        pivot = jnp.sum(jnp.where(across[:1] == t, row_a, 0.0), axis=1, keepdims=True)
        row_a = row_a / pivot
        row_b = row_b / pivot
        return (
            jnp.where(down == t, row_a, a - column * row_a),
            jnp.where(down_right == t, row_b, b - column * row_b),
        )

    return lax.fori_loop(0, intervals, eliminate, (normal, right))[1]


def kernel(
    dates,
    mates,
    group,
    frames,
    heights,
    spacings,
    flags_scalar,
    flags_vector,
    targets,
    totals,
    coherence,
    velocities,
    held,
    height_rows,
    natural,
    height_looks,
    rotated,
    powers,
    phases,
    coh,
    gathered,
    gathered_late,
    partial,
    partials,
    send_sem,
    recv_sem,
    coh_send_sem,
    coh_recv_sem,
    late_send_sem,
    late_recv_sem,
    part_send_sem,
    part_recv_sem,
    local_sem,
):
    me = lax.axis_index("tile")
    g = me // group
    q = me % group
    groups = dates // group
    share = dates // group
    half = share // 2
    cols = held.shape[3]
    rows = held.shape[2] // share
    tiles = cols // LANES
    looks = rows // LOOK_ROWS
    looked_cols = cols // LOOK_COLS
    slots = targets.shape[1]
    window = rotated.shape[0]
    base = g * group - mates
    own_slot = q + mates

    def share_rows(member, first, count, unit):
        return pl.ds(pl.multiple_of((member * share + first) * unit, unit), count * unit)

    own_block = pltpu.make_async_copy(
        frames.at[0, :, share_rows(q, 0, share, rows), :], held.at[own_slot], local_sem.at[0]
    )
    own_heights = pltpu.make_async_copy(
        heights.at[share_rows(q, 0, share, rows), :], height_rows, local_sem.at[1]
    )
    own_block.start()
    own_heights.start()
    gathered_late[...] = jnp.zeros_like(gathered_late)

    barrier = pltpu.get_barrier_semaphore()

    def greet(step, carry):
        pl.semaphore_signal(
            barrier,
            inc=1,
            device_id={"tile": (me + step) % dates},
            device_id_type=pl.DeviceIdType.MESH,
        )
        return carry

    lax.fori_loop(1, dates, greet, 0)
    pl.semaphore_wait(barrier, dates - 1)

    def remote(src, dst, send, recv, to):
        return pltpu.make_async_remote_copy(
            src_ref=src,
            dst_ref=dst,
            send_sem=send,
            recv_sem=recv,
            device_id={"tile": to},
            device_id_type=pl.DeviceIdType.MESH,
        )

    def image_copy(member, slot, part):
        return remote(
            frames.at[0, :, share_rows(member, part * half, half, rows), :],
            held.at[slot, :, pl.ds(part * half * rows, half * rows), :],
            send_sem.at[1 + part, member],
            recv_sem.at[part, slot],
            g * group + member,
        )

    def to_previous(member):
        return remote(
            frames.at[0, :, share_rows(member, 0, half, rows), :],
            held.at[q + group + mates, :, pl.ds(0, half * rows), :],
            send_sem.at[0, member],
            recv_sem.at[0, q + group + mates],
            (g - 1) * group + member,
        )

    def to_next(member):
        return remote(
            frames.at[0, :, share_rows(member, half, share - half, rows), :],
            held.at[q - group + mates, :, pl.ds(half * rows, (share - half) * rows), :],
            send_sem.at[3, member],
            recv_sem.at[1, q - group + mates],
            (g + 1) * group + member,
        )

    def arrival(slot, part):
        place = held.at[slot, :, pl.ds(part * half * rows, half * rows), :]
        return remote(place, place, send_sem.at[0, 0], recv_sem.at[part, slot], (me + 1) % dates)

    feeds_previous = (g > 0) & (q < mates)
    feeds_next = (g < groups - 1) & (q >= group - mates)

    def partner(step):
        return q ^ step if group & (group - 1) == 0 else (q + step) % group

    @pl.when(feeds_previous)
    def _():
        lax.fori_loop(0, group, lambda member, carry: (to_previous(member).start(), carry)[1], 0)

    lax.fori_loop(
        1,
        group,
        lambda step, carry: (image_copy(partner(group - step), own_slot, 0).start(), carry)[1],
        0,
    )

    @pl.when(feeds_next)
    def _():
        lax.fori_loop(0, group, lambda member, carry: (to_next(member).start(), carry)[1], 0)

    lax.fori_loop(
        1,
        group,
        lambda step, carry: (image_copy(partner(group - step), own_slot, 1).start(), carry)[1],
        0,
    )

    rotated[...] = jnp.zeros_like(rotated)
    powers[...] = jnp.zeros_like(powers)
    phases[...] = jnp.zeros_like(phases)
    coh[...] = jnp.zeros_like(coh)
    assert mates * looked_cols <= LANES

    mapping = inverse_map(flags_vector[...], dates, mates)

    look_lane = iota((cols, LANES), 1)
    pooling = jnp.where(
        iota((cols, LANES), 0) // LOOK_COLS == look_lane, 1.0 / (LOOK_ROWS * LOOK_COLS), 0.0
    ).astype(jnp.bfloat16)

    kept = phases.shape[1]
    offset = base * mates
    expand = jnp.where(
        iota((mapping.shape[1], kept * looks), 1) // looks + offset
        == iota((mapping.shape[1], kept * looks), 0),
        1.0,
        0.0,
    )
    wide = jnp.dot(mapping, expand, precision=HIGHEST, preferred_element_type=jnp.float32)

    def part_copy(tile, source, to):
        return remote(
            partial.at[tile],
            partials.at[source],
            part_send_sem.at[tile],
            part_recv_sem.at[source],
            to,
        )

    def own_part(tile):
        return pltpu.make_async_copy(partial.at[tile], partials.at[g], local_sem.at[3])

    def pick(tile):
        whole_tile = q * share + tile
        listed = targets[pl.ds(whole_tile, 1), :]
        diagonal = iota((slots, slots), 0) == iota((slots, slots), 1)
        row_of = (listed // looked_cols).astype(jnp.float32)
        column_of = (listed % looked_cols).astype(jnp.float32)
        row_down = jnp.sum(jnp.where(diagonal, row_of, 0.0), axis=1, keepdims=True)
        column_down = jnp.sum(jnp.where(diagonal, column_of, 0.0), axis=1, keepdims=True)
        by_column = jnp.where(
            iota((slots, LANES), 1).astype(jnp.float32) == column_down, 1.0, 0.0
        )
        flat_phases = phases[tile].reshape(kept * looks, LANES)
        rows_picked = lax.dot_general(
            by_column,
            flat_phases,
            (((1,), (1,)), ((), ())),
            precision=HIGHEST,
            preferred_element_type=jnp.float32,
        )
        lane = iota((slots, kept * looks), 1)
        picked = jnp.where((lane % looks).astype(jnp.float32) == row_down, rows_picked, 0.0)
        result = lax.dot_general(
            wide,
            picked,
            (((1,), (1,)), ((), ())),
            precision=HIGHEST,
            preferred_element_type=jnp.float32,
        )
        partial[tile] = jnp.where(iota(result.shape, 1) < totals[whole_tile], result, 0.0)

        @pl.when(whole_tile == me)
        def _():
            own_part(tile).start()

        @pl.when(whole_tile != me)
        def _():
            part_copy(tile, g, whole_tile).start()

    own_block.wait()
    own_heights.wait()

    def one_tile(tile, carry):
        lower = tile // half
        tile_rows = pl.ds(pl.multiple_of(tile * rows, rows), rows)
        tile_looks = pl.ds(pl.multiple_of(tile * looks, looks), looks)
        for c in range(tiles):
            natural[0, c] = height_rows[tile_rows, c * LANES : (c + 1) * LANES]
        for j in range(LOOK_ROWS):
            height_looks[j] = natural[0, :, pl.ds(j, looks, stride=LOOK_ROWS), :]

        def one_date(step, carry):
            slot = step + mates * (1 - lower)
            date = base + slot

            @pl.when((date >= 0) & (date <= dates))
            def _():
                visit(step, slot, date)

            return carry

        def visit(step, slot, date):
            real_date = (step < group + mates) & (date < dates)

            @pl.when(real_date & (tile == 0) & (slot != own_slot))
            def _():
                arrival(slot, 0).wait_recv()

            @pl.when(real_date & (tile == half) & (slot != own_slot))
            def _():
                arrival(slot, 1).wait_recv()

            before = slot + window - 1
            place = before % window
            fields = []
            for k in range(1, mates + 1):
                other = (before + window - k) % window
                flat_real = 0.0
                flat_imag = 0.0
                for j in range(LOOK_ROWS):
                    a_real = rotated[other, 0, j]
                    a_imag = rotated[other, 1, j]
                    c_real = rotated[place, 0, j]
                    c_imag = rotated[place, 1, j]
                    flat_real = flat_real + (a_real * c_real + a_imag * c_imag)
                    flat_imag = flat_imag + (a_imag * c_real - a_real * c_imag)
                fields += [flat_real, flat_imag]
            for plane in range(2):
                for c in range(tiles):
                    natural[plane, c] = held[
                        slot - step // (group + mates), plane, tile_rows, c * LANES : (c + 1) * LANES
                    ].astype(jnp.float32)
            spacing = spacings[date - date // dates]
            power = None
            for j in range(LOOK_ROWS):
                real = natural[0, :, pl.ds(j, looks, stride=LOOK_ROWS), :]
                imag = natural[1, :, pl.ds(j, looks, stride=LOOK_ROWS), :]
                sine, cosine = sine_cosine(spacing * height_looks[j])
                rotated[slot % window, 0, j] = real * cosine + imag * sine
                rotated[slot % window, 1, j] = imag * cosine - real * sine
                energy = real * real + imag * imag
                power = energy if j == 0 else power + energy
            fields = [power] + fields
            sums = jnp.concatenate(
                [jnp.concatenate([field[c] for c in range(tiles)], axis=1) for field in fields],
                axis=0,
            )
            high = sums.astype(jnp.bfloat16).astype(jnp.float32)
            split = jnp.concatenate([high, sums - high], axis=0).astype(jnp.bfloat16)
            pooled = jnp.dot(split, pooling, preferred_element_type=jnp.float32)
            means = pooled[: sums.shape[0]] + pooled[sums.shape[0] :]
            power_other = powers[place]
            power_next = means[:looks]
            for k in range(1, mates + 1):
                mean_real = means[(2 * k - 1) * looks : 2 * k * looks]
                mean_imag = means[2 * k * looks : (2 * k + 1) * looks]
                power_own = powers[(before + window - k) % window]
                scale = 1.0 / jnp.sqrt(power_own * power_other + EPSILON)
                amplitude = jnp.sqrt(mean_real * mean_real + mean_imag * mean_imag) * scale

                @pl.when((step > k) & (date > k) & (slot > mates) & (slot - k <= group + mates))
                def _():
                    flag = flags_scalar[k - 1, date - 1 - k].astype(jnp.float32)
                    shown = amplitude * flag
                    if k > 1:
                        shown = pltpu.roll(shown, (k - 1) * looked_cols, 1)
                    coh[slot - 1 - k, tile_looks, :] = coh[slot - 1 - k, tile_looks, :] + shown
                    phases[tile, (slot - 1 - k) * mates + (k - 1)] = mean_imag * scale

            powers[slot % window] = power_next

        lax.fori_loop(0, group + mates + 1, one_date, 0)

        @pl.when(tile < share - 1)
        def _():
            pick(tile)

        return carry

    lax.fori_loop(0, share, one_tile, 0)

    def coh_copy(to, member):
        return remote(
            coh.at[to + mates],
            gathered.at[share_rows(member, 0, share, looks), :],
            coh_send_sem.at[to],
            coh_recv_sem.at[member],
            g * group + to,
        )

    def late_copy(slot, member):
        return remote(
            coh.at[slot, pl.ds(half * looks, (share - half) * looks), :],
            gathered_late.at[share_rows(member, half, share - half, looks), :],
            late_send_sem.at[slot],
            late_recv_sem.at[member],
            (base + slot + dates) % dates,
        )

    own_coh = pltpu.make_async_copy(
        coh.at[own_slot], gathered.at[share_rows(q, 0, share, looks), :], local_sem.at[2]
    )
    own_coh.start()
    lax.fori_loop(
        1, group, lambda step, carry: (coh_copy(partner(group - step), q).start(), carry)[1], 0
    )

    @pl.when(g > 0)
    def _():
        lax.fori_loop(0, mates, lambda slot, carry: (late_copy(slot, q).start(), carry)[1], 0)

    pick(share - 1)

    own_coh.wait()

    def finish(step, carry):
        other = (q + step) % group
        image_copy(other, own_slot, 0).wait_send()
        image_copy(other, own_slot, 1).wait_send()
        coh_copy(other, q).wait_send()
        coh_copy(other, other).wait_recv()
        return carry

    lax.fori_loop(1, group, finish, 0)

    def finish_beyond(member, carry):
        @pl.when(feeds_previous)
        def _():
            to_previous(member).wait_send()

        @pl.when(feeds_next)
        def _():
            to_next(member).wait_send()
            late_copy(0, member).wait_recv()

        return carry

    lax.fori_loop(0, group, finish_beyond, 0)

    @pl.when(g > 0)
    def _():
        lax.fori_loop(0, mates, lambda slot, carry: (late_copy(slot, q).wait_send(), carry)[1], 0)

    across_rows = jnp.transpose(gathered[...] + gathered_late[...])
    for k in range(mates):
        coherence[0, k] = across_rows[k * looked_cols : (k + 1) * looked_cols]

    def finish_part(tile, carry):
        whole_tile = q * share + tile

        @pl.when(whole_tile == me)
        def _():
            own_part(tile).wait()

        @pl.when(whole_tile != me)
        def _():
            part_copy(tile, g, whole_tile).wait_send()

        return carry

    lax.fori_loop(0, share, finish_part, 0)

    def arrive(source, carry):
        @pl.when(source * group + me // share != me)
        def _():
            part_copy(0, source, (me + 1) % dates).wait_recv()

        return carry

    lax.fori_loop(0, groups, arrive, 0)
    velocities[...] = jnp.sum(partials[...], axis=0)[: dates - 1]


def local(
    full_resolution_frames,
    height_angle_factor,
    normal_spacings,
    couple_entry_flags,
    block_target_indices,
    block_target_totals,
):
    dates, mates = couple_entry_flags.shape
    image_rows, cols = height_angle_factor.shape
    group = 8
    share = dates // group
    assert dates % group == 0 and share % 2 == 0
    rows = image_rows // dates
    tiles = cols // LANES
    looks = rows // LOOK_ROWS
    looked_cols = cols // LOOK_COLS
    slots = block_target_indices.shape[1]
    window = mates + 2
    padded = -(-(dates - 1) // 8) * 8
    f32 = jnp.float32
    vmem = pl.BlockSpec(memory_space=pltpu.VMEM)
    smem = pl.BlockSpec(memory_space=pltpu.SMEM)
    hbm = pl.BlockSpec(memory_space=pltpu.HBM)
    coherence, velocities = pl.pallas_call(
        functools.partial(kernel, dates, mates, group),
        out_shape=(
            jax.ShapeDtypeStruct((1, mates, looked_cols, image_rows // LOOK_ROWS), f32),
            jax.ShapeDtypeStruct((dates - 1, slots), f32),
        ),
        in_specs=[hbm, hbm, smem, smem, vmem, vmem, smem],
        out_specs=(vmem, vmem),
        scratch_shapes=[
            pltpu.VMEM((group + 2 * mates, 2, share * rows, cols), jnp.bfloat16),
            pltpu.VMEM((share * rows, cols), f32),
            pltpu.VMEM((2, tiles, rows, LANES), f32),
            pltpu.VMEM((LOOK_ROWS, tiles, looks, LANES), f32),
            pltpu.VMEM((window, 2, LOOK_ROWS, tiles, looks, LANES), f32),
            pltpu.VMEM((window, looks, LANES), f32),
            pltpu.VMEM((share, (group + mates) * mates, looks, LANES), f32),
            pltpu.VMEM((group + mates, share * looks, LANES), f32),
            pltpu.VMEM((image_rows // LOOK_ROWS, LANES), f32),
            pltpu.VMEM((image_rows // LOOK_ROWS, LANES), f32),
            pltpu.VMEM((share, padded, slots), f32),
            pltpu.VMEM((dates // group, padded, slots), f32),
            pltpu.SemaphoreType.DMA((4, group)),
            pltpu.SemaphoreType.DMA((2, group + 2 * mates)),
            pltpu.SemaphoreType.DMA((group,)),
            pltpu.SemaphoreType.DMA((group,)),
            pltpu.SemaphoreType.DMA((mates,)),
            pltpu.SemaphoreType.DMA((group,)),
            pltpu.SemaphoreType.DMA((share,)),
            pltpu.SemaphoreType.DMA((dates // group,)),
            pltpu.SemaphoreType.DMA((4,)),
        ],
        compiler_params=pltpu.CompilerParams(
            collective_id=0, has_side_effects=True, vmem_limit_bytes=62 * 1024 * 1024
        ),
    )(
        full_resolution_frames,
        height_angle_factor,
        normal_spacings,
        couple_entry_flags.T,
        couple_entry_flags.T,
        block_target_indices,
        block_target_totals,
    )
    return jnp.swapaxes(coherence, 2, 3), velocities.T


def solution(mesh):
    in_specs = (
        P(("grp", "tile"), None, None, None),
        P("grp", None),
        P("grp"),
        P(),
        P("grp", None),
        P("grp"),
    )
    out_specs = (P(("grp", "tile"), None, None, None), P(("grp", "tile"), None))
    return jax.shard_map(local, mesh=mesh, in_specs=in_specs, out_specs=out_specs, check_vma=False)
```

```python
import functools

import jax
import jax.numpy as jnp
from jax import lax
from jax.experimental import pallas as pl
from jax.experimental.pallas import tpu as pltpu
from jax.sharding import PartitionSpec as P

LOOK_ROWS = 4
LOOK_COLS = 16
LANES = 128
EPSILON = 1e-06
HIGHEST = lax.Precision.HIGHEST


def iota(shape, axis):
    return lax.broadcasted_iota(jnp.int32, shape, axis)


def sine_cosine(x):
    turns = jnp.round(x * 0.6366197723675814)
    r = (x - turns * 1.5703125) - turns * 4.838267948966e-4
    z = r * r
    s = r + r * z * (-1.6666654611e-1 + z * (8.3321608736e-3 + z * -1.9515295891e-4))
    c = 1.0 - 0.5 * z + z * z * (
        4.166664568298827e-2 + z * (-1.388731625493765e-3 + z * 2.443315711809948e-5)
    )
    quarter = turns.astype(jnp.int32)
    odd = (quarter & 1) == 1
    sine = jnp.where(odd, c, s) * (1 - (quarter & 2)).astype(jnp.float32)
    cosine = jnp.where(odd, s, c) * (1 - ((quarter + 1) & 2)).astype(jnp.float32)
    return sine, cosine


def inverse_map(flags, dates, mates):
    intervals = dates - 1
    rows = -(-intervals // 8) * 8
    pairs = -(-dates * mates // LANES) * LANES
    own_slot = iota((dates, pairs), 1) // mates == iota((dates, pairs), 0)
    spread = jnp.dot(
        flags.astype(jnp.bfloat16),
        jnp.where(own_slot, 1.0, 0.0).astype(jnp.bfloat16),
        preferred_element_type=jnp.float32,
    )
    kind = iota((mates, pairs), 1) % mates == iota((mates, pairs), 0)
    used = jnp.sum(jnp.where(kind, spread, 0.0), axis=0, keepdims=True)
    interval = iota((rows, pairs), 0)
    pair = iota((rows, pairs), 1)
    first = pair // mates
    covered = (interval >= first) & (interval < first + pair % mates + 1) & (interval < intervals)
    right = jnp.where(covered, used, 0.0)
    normal = lax.dot_general(
        right.astype(jnp.bfloat16),
        right.astype(jnp.bfloat16),
        (((1,), (1,)), ((), ())),
        preferred_element_type=jnp.float32,
    )
    down = iota((rows, rows), 0)
    across = iota((rows, rows), 1)
    down_right = iota((rows, pairs), 0)

    def eliminate(t, carry):
        a, b = carry
        row_a = jnp.sum(jnp.where(down == t, a, 0.0), axis=0, keepdims=True)
        row_b = jnp.sum(jnp.where(down_right == t, b, 0.0), axis=0, keepdims=True)
        column = jnp.sum(jnp.where(across == t, a, 0.0), axis=1, keepdims=True)
        pivot = jnp.sum(jnp.where(across[:1] == t, row_a, 0.0), axis=1, keepdims=True)
        row_a = row_a / pivot
        row_b = row_b / pivot
        return (
            jnp.where(down == t, row_a, a - column * row_a),
            jnp.where(down_right == t, row_b, b - column * row_b),
        )

    return lax.fori_loop(0, intervals, eliminate, (normal, right))[1]


def kernel(
    dates,
    mates,
    group,
    frames,
    heights,
    spacings,
    flags_scalar,
    flags_vector,
    targets,
    totals,
    coherence,
    velocities,
    held,
    height_rows,
    natural,
    height_looks,
    rotated,
    powers,
    phases,
    coh,
    gathered,
    gathered_late,
    partial,
    partials,
    send_sem,
    recv_sem,
    coh_send_sem,
    coh_recv_sem,
    late_send_sem,
    late_recv_sem,
    part_send_sem,
    part_recv_sem,
    local_sem,
):
    me = lax.axis_index("tile")
    g = me // group
    q = me % group
    groups = dates // group
    share = dates // group
    half = share // 2
    cols = held.shape[3]
    rows = held.shape[2] // share
    tiles = cols // LANES
    looks = rows // LOOK_ROWS
    looked_cols = cols // LOOK_COLS
    slots = targets.shape[1]
    window = rotated.shape[0]
    base = g * group - mates
    own_slot = q + mates

    def share_rows(member, first, count, unit):
        return pl.ds(pl.multiple_of((member * share + first) * unit, unit), count * unit)

    own_block = pltpu.make_async_copy(
        frames.at[0, :, share_rows(q, 0, share, rows), :], held.at[own_slot], local_sem.at[0]
    )
    own_heights = pltpu.make_async_copy(
        heights.at[share_rows(q, 0, share, rows), :], height_rows, local_sem.at[1]
    )
    own_block.start()
    own_heights.start()
    gathered_late[...] = jnp.zeros_like(gathered_late)

    barrier = pltpu.get_barrier_semaphore()

    def greet(step, carry):
        pl.semaphore_signal(
            barrier,
            inc=1,
            device_id={"tile": (me + step) % dates},
            device_id_type=pl.DeviceIdType.MESH,
        )
        return carry

    lax.fori_loop(1, dates, greet, 0)
    pl.semaphore_wait(barrier, dates - 1)

    def remote(src, dst, send, recv, to):
        return pltpu.make_async_remote_copy(
            src_ref=src,
            dst_ref=dst,
            send_sem=send,
            recv_sem=recv,
            device_id={"tile": to},
            device_id_type=pl.DeviceIdType.MESH,
        )

    def image_copy(member, slot, part):
        return remote(
            frames.at[0, :, share_rows(member, part * half, half, rows), :],
            held.at[slot, :, pl.ds(part * half * rows, half * rows), :],
            send_sem.at[1 + part, member],
            recv_sem.at[part, slot],
            g * group + member,
        )

    def to_previous(member):
        return remote(
            frames.at[0, :, share_rows(member, 0, half, rows), :],
            held.at[q + group + mates, :, pl.ds(0, half * rows), :],
            send_sem.at[0, member],
            recv_sem.at[0, q + group + mates],
            (g - 1) * group + member,
        )

    def to_next(member):
        return remote(
            frames.at[0, :, share_rows(member, half, share - half, rows), :],
            held.at[q - group + mates, :, pl.ds(half * rows, (share - half) * rows), :],
            send_sem.at[3, member],
            recv_sem.at[1, q - group + mates],
            (g + 1) * group + member,
        )

    def arrival(slot, part):
        place = held.at[slot, :, pl.ds(part * half * rows, half * rows), :]
        return remote(place, place, send_sem.at[0, 0], recv_sem.at[part, slot], (me + 1) % dates)

    feeds_previous = (g > 0) & (q < mates)
    feeds_next = (g < groups - 1) & (q >= group - mates)

    def partner(step):
        return q ^ step if group & (group - 1) == 0 else (q + step) % group

    @pl.when(feeds_previous)
    def _():
        lax.fori_loop(0, group, lambda member, carry: (to_previous(member).start(), carry)[1], 0)

    lax.fori_loop(
        1,
        group,
        lambda step, carry: (image_copy(partner(group - step), own_slot, 0).start(), carry)[1],
        0,
    )

    @pl.when(feeds_next)
    def _():
        lax.fori_loop(0, group, lambda member, carry: (to_next(member).start(), carry)[1], 0)

    lax.fori_loop(
        1,
        group,
        lambda step, carry: (image_copy(partner(group - step), own_slot, 1).start(), carry)[1],
        0,
    )

    rotated[...] = jnp.zeros_like(rotated)
    powers[...] = jnp.zeros_like(powers)
    phases[...] = jnp.zeros_like(phases)
    coh[...] = jnp.zeros_like(coh)
    assert mates * looked_cols <= LANES

    mapping = inverse_map(flags_vector[...], dates, mates)

    look_lane = iota((cols, LANES), 1)
    pooling = jnp.where(
        iota((cols, LANES), 0) // LOOK_COLS == look_lane, 1.0 / (LOOK_ROWS * LOOK_COLS), 0.0
    ).astype(jnp.bfloat16)

    kept = phases.shape[1]
    offset = base * mates
    expand = jnp.where(
        iota((mapping.shape[1], kept * looks), 1) // looks + offset
        == iota((mapping.shape[1], kept * looks), 0),
        1.0,
        0.0,
    )
    wide = jnp.dot(mapping, expand, precision=HIGHEST, preferred_element_type=jnp.float32)

    def part_copy(tile, source, to):
        return remote(
            partial.at[tile],
            partials.at[source],
            part_send_sem.at[tile],
            part_recv_sem.at[source],
            to,
        )

    def own_part(tile):
        return pltpu.make_async_copy(partial.at[tile], partials.at[g], local_sem.at[3])

    def pick(tile):
        whole_tile = q * share + tile
        listed = targets[pl.ds(whole_tile, 1), :]
        diagonal = iota((slots, slots), 0) == iota((slots, slots), 1)
        row_of = (listed // looked_cols).astype(jnp.float32)
        column_of = (listed % looked_cols).astype(jnp.float32)
        row_down = jnp.sum(jnp.where(diagonal, row_of, 0.0), axis=1, keepdims=True)
        column_down = jnp.sum(jnp.where(diagonal, column_of, 0.0), axis=1, keepdims=True)
        by_column = jnp.where(
            iota((slots, LANES), 1).astype(jnp.float32) == column_down, 1.0, 0.0
        )
        flat_phases = phases[tile].reshape(kept * looks, LANES)
        rows_picked = lax.dot_general(
            by_column,
            flat_phases,
            (((1,), (1,)), ((), ())),
            precision=HIGHEST,
            preferred_element_type=jnp.float32,
        )
        lane = iota((slots, kept * looks), 1)
        picked = jnp.where((lane % looks).astype(jnp.float32) == row_down, rows_picked, 0.0)
        result = lax.dot_general(
            wide,
            picked,
            (((1,), (1,)), ((), ())),
            precision=HIGHEST,
            preferred_element_type=jnp.float32,
        )
        partial[tile] = jnp.where(iota(result.shape, 1) < totals[whole_tile], result, 0.0)

        @pl.when(whole_tile == me)
        def _():
            own_part(tile).start()

        @pl.when(whole_tile != me)
        def _():
            part_copy(tile, g, whole_tile).start()

    own_block.wait()
    own_heights.wait()

    def one_tile(tile, carry):
        lower = tile // half
        tile_rows = pl.ds(pl.multiple_of(tile * rows, rows), rows)
        tile_looks = pl.ds(pl.multiple_of(tile * looks, looks), looks)
        for c in range(tiles):
            natural[0, c] = height_rows[tile_rows, c * LANES : (c + 1) * LANES]
        for j in range(LOOK_ROWS):
            height_looks[j] = natural[0, :, pl.ds(j, looks, stride=LOOK_ROWS), :]

        def one_date(step, carry):
            slot = step + mates * (1 - lower)
            date = base + slot

            @pl.when((date >= 0) & (date < dates))
            def _():
                visit(step, slot, date)

            return carry

        def visit(step, slot, date):
            @pl.when((tile == 0) & (slot != own_slot))
            def _():
                arrival(slot, 0).wait_recv()

            @pl.when((tile == half) & (slot != own_slot))
            def _():
                arrival(slot, 1).wait_recv()

            place = slot % window
            for plane in range(2):
                for c in range(tiles):
                    natural[plane, c] = held[
                        slot, plane, tile_rows, c * LANES : (c + 1) * LANES
                    ].astype(jnp.float32)
            spacing = spacings[date]
            power = None
            for j in range(LOOK_ROWS):
                real = natural[0, :, pl.ds(j, looks, stride=LOOK_ROWS), :]
                imag = natural[1, :, pl.ds(j, looks, stride=LOOK_ROWS), :]
                sine, cosine = sine_cosine(spacing * height_looks[j])
                rotated[place, 0, j] = real * cosine + imag * sine
                rotated[place, 1, j] = imag * cosine - real * sine
                energy = real * real + imag * imag
                power = energy if j == 0 else power + energy
            fields = [power]
            for k in range(1, mates + 1):
                other = (slot + window - k) % window
                flat_real = 0.0
                flat_imag = 0.0
                for j in range(LOOK_ROWS):
                    a_real = rotated[other, 0, j]
                    a_imag = rotated[other, 1, j]
                    c_real = rotated[place, 0, j]
                    c_imag = rotated[place, 1, j]
                    flat_real = flat_real + (a_real * c_real + a_imag * c_imag)
                    flat_imag = flat_imag + (a_imag * c_real - a_real * c_imag)
                fields += [flat_real, flat_imag]
            sums = jnp.concatenate(
                [jnp.concatenate([field[c] for c in range(tiles)], axis=1) for field in fields],
                axis=0,
            )
            high = sums.astype(jnp.bfloat16).astype(jnp.float32)
            split = jnp.concatenate([high, sums - high], axis=0).astype(jnp.bfloat16)
            pooled = jnp.dot(split, pooling, preferred_element_type=jnp.float32)
            means = pooled[: sums.shape[0]] + pooled[sums.shape[0] :]
            power_other = means[:looks]
            powers[place] = power_other
            for k in range(1, mates + 1):
                mean_real = means[(2 * k - 1) * looks : 2 * k * looks]
                mean_imag = means[2 * k * looks : (2 * k + 1) * looks]
                power_own = powers[(slot + window - k) % window]
                scale = lax.rsqrt(power_own * power_other + EPSILON)
                amplitude = jnp.sqrt(mean_real * mean_real + mean_imag * mean_imag) * scale

                @pl.when((step >= k) & (date >= k) & (slot >= mates) & (slot - k < group + mates))
                def _():
                    flag = flags_scalar[k - 1, date - k].astype(jnp.float32)
                    shown = amplitude * flag
                    if k > 1:
                        shown = pltpu.roll(shown, (k - 1) * looked_cols, 1)
                    coh[slot - k, tile_looks, :] = coh[slot - k, tile_looks, :] + shown
                    phases[tile, (slot - k) * mates + (k - 1)] = mean_imag * scale

        lax.fori_loop(0, group + mates, one_date, 0)

        @pl.when(tile < share - 1)
        def _():
            pick(tile)

        return carry

    lax.fori_loop(0, share, one_tile, 0)

    def coh_copy(to, member):
        return remote(
            coh.at[to + mates],
            gathered.at[share_rows(member, 0, share, looks), :],
            coh_send_sem.at[to],
            coh_recv_sem.at[member],
            g * group + to,
        )

    def late_copy(slot, member):
        return remote(
            coh.at[slot, pl.ds(half * looks, (share - half) * looks), :],
            gathered_late.at[share_rows(member, half, share - half, looks), :],
            late_send_sem.at[slot],
            late_recv_sem.at[member],
            (base + slot + dates) % dates,
        )

    own_coh = pltpu.make_async_copy(
        coh.at[own_slot], gathered.at[share_rows(q, 0, share, looks), :], local_sem.at[2]
    )
    own_coh.start()
    lax.fori_loop(
        1, group, lambda step, carry: (coh_copy(partner(group - step), q).start(), carry)[1], 0
    )

    @pl.when(g > 0)
    def _():
        lax.fori_loop(0, mates, lambda slot, carry: (late_copy(slot, q).start(), carry)[1], 0)

    pick(share - 1)

    own_coh.wait()

    def finish(step, carry):
        other = (q + step) % group
        image_copy(other, own_slot, 0).wait_send()
        image_copy(other, own_slot, 1).wait_send()
        coh_copy(other, q).wait_send()
        coh_copy(other, other).wait_recv()
        return carry

    lax.fori_loop(1, group, finish, 0)

    def finish_beyond(member, carry):
        @pl.when(feeds_previous)
        def _():
            to_previous(member).wait_send()

        @pl.when(feeds_next)
        def _():
            to_next(member).wait_send()
            late_copy(0, member).wait_recv()

        return carry

    lax.fori_loop(0, group, finish_beyond, 0)

    @pl.when(g > 0)
    def _():
        lax.fori_loop(0, mates, lambda slot, carry: (late_copy(slot, q).wait_send(), carry)[1], 0)

    across_rows = jnp.transpose(gathered[...] + gathered_late[...])
    for k in range(mates):
        coherence[0, k] = across_rows[k * looked_cols : (k + 1) * looked_cols]

    def finish_part(tile, carry):
        whole_tile = q * share + tile

        @pl.when(whole_tile == me)
        def _():
            own_part(tile).wait()

        @pl.when(whole_tile != me)
        def _():
            part_copy(tile, g, whole_tile).wait_send()

        return carry

    lax.fori_loop(0, share, finish_part, 0)

    def arrive(source, carry):
        @pl.when(source * group + me // share != me)
        def _():
            part_copy(0, source, (me + 1) % dates).wait_recv()

        return carry

    lax.fori_loop(0, groups, arrive, 0)
    velocities[...] = jnp.sum(partials[...], axis=0)[: dates - 1]


def local(
    full_resolution_frames,
    height_angle_factor,
    normal_spacings,
    couple_entry_flags,
    block_target_indices,
    block_target_totals,
):
    dates, mates = couple_entry_flags.shape
    image_rows, cols = height_angle_factor.shape
    group = 8
    share = dates // group
    assert dates % group == 0 and share % 2 == 0
    rows = image_rows // dates
    tiles = cols // LANES
    looks = rows // LOOK_ROWS
    looked_cols = cols // LOOK_COLS
    slots = block_target_indices.shape[1]
    window = mates + 1
    padded = -(-(dates - 1) // 8) * 8
    f32 = jnp.float32
    vmem = pl.BlockSpec(memory_space=pltpu.VMEM)
    smem = pl.BlockSpec(memory_space=pltpu.SMEM)
    hbm = pl.BlockSpec(memory_space=pltpu.HBM)
    coherence, velocities = pl.pallas_call(
        functools.partial(kernel, dates, mates, group),
        out_shape=(
            jax.ShapeDtypeStruct((1, mates, looked_cols, image_rows // LOOK_ROWS), f32),
            jax.ShapeDtypeStruct((dates - 1, slots), f32),
        ),
        in_specs=[hbm, hbm, smem, smem, vmem, vmem, smem],
        out_specs=(vmem, vmem),
        scratch_shapes=[
            pltpu.VMEM((group + 2 * mates, 2, share * rows, cols), jnp.bfloat16),
            pltpu.VMEM((share * rows, cols), f32),
            pltpu.VMEM((2, tiles, rows, LANES), f32),
            pltpu.VMEM((LOOK_ROWS, tiles, looks, LANES), f32),
            pltpu.VMEM((window, 2, LOOK_ROWS, tiles, looks, LANES), f32),
            pltpu.VMEM((window, looks, LANES), f32),
            pltpu.VMEM((share, (group + mates) * mates, looks, LANES), f32),
            pltpu.VMEM((group + mates, share * looks, LANES), f32),
            pltpu.VMEM((image_rows // LOOK_ROWS, LANES), f32),
            pltpu.VMEM((image_rows // LOOK_ROWS, LANES), f32),
            pltpu.VMEM((share, padded, slots), f32),
            pltpu.VMEM((dates // group, padded, slots), f32),
            pltpu.SemaphoreType.DMA((4, group)),
            pltpu.SemaphoreType.DMA((2, group + 2 * mates)),
            pltpu.SemaphoreType.DMA((group,)),
            pltpu.SemaphoreType.DMA((group,)),
            pltpu.SemaphoreType.DMA((mates,)),
            pltpu.SemaphoreType.DMA((group,)),
            pltpu.SemaphoreType.DMA((share,)),
            pltpu.SemaphoreType.DMA((dates // group,)),
            pltpu.SemaphoreType.DMA((4,)),
        ],
        compiler_params=pltpu.CompilerParams(
            collective_id=0, has_side_effects=True, vmem_limit_bytes=62 * 1024 * 1024
        ),
    )(
        full_resolution_frames,
        height_angle_factor,
        normal_spacings,
        couple_entry_flags.T,
        couple_entry_flags.T,
        block_target_indices,
        block_target_totals,
    )
    return jnp.swapaxes(coherence, 2, 3), velocities.T


def solution(mesh):
    in_specs = (
        P(("grp", "tile"), None, None, None),
        P("grp", None),
        P("grp"),
        P(),
        P("grp", None),
        P("grp"),
    )
    out_specs = (P(("grp", "tile"), None, None, None), P(("grp", "tile"), None))
    return jax.shard_map(local, mesh=mesh, in_specs=in_specs, out_specs=out_specs, check_vma=False)
```
